512 devices in a mesh: sect: 2 (over core), exp: 64 (over y, z), lat: 4 (over x).
Axes of the slice: x: 4, y: 4, z: 16, core: 2. Of those that a mesh axis runs over, the one named last changes fastest.
Arguments:
- residuals: bfloat16 [16384, 4608], P(('sect', 'exp'), 'lat'), may hold values from -6 to 6
- routes: int32 [16384], P(('sect', 'exp')), may hold values from 0 to 3, as said below
- blocks: int32 [16384, 4], P(('sect', 'exp')), may hold values from 0 to 63, as said below
- enc_weight: bfloat16 [256, 128, 4608], P(('sect', 'exp'), None, 'lat'), may hold values from -0.09375 to 0.09375
- enc_bias: float32 [256, 128], P(('sect', 'exp')), may hold values from -3 to 3
- dec_weight: bfloat16 [256, 128, 4608], P(('sect', 'exp'), None, 'lat'), may hold values from -0.25 to 0.25
- dec_bias: float32 [4608], P('lat'), may hold values from -3 to 3
Outputs:
- reconstruction: bfloat16 [16384, 4608], P(('sect', 'exp'), 'lat')
- enc_grad: bfloat16 [256, 128, 4608], P(('sect', 'exp'), None, 'lat')
- enc_bias_grad: float32 [256, 128], P(('sect', 'exp'))
- dec_grad: bfloat16 [256, 128, 4608], P(('sect', 'exp'), None, 'lat')
The draws below stay inside these ranges and needn't reach their ends.
Inputs may be any that keep to these rules, and one draw needn't show every extreme that they name: `routes`: half of the tokens of each index of sect and exp route to one expert of that index; the rest route to the other experts. A token's 4 blocks are distinct. Among the 128 tokens of one index of sect and exp, no global block is named by more than 4 of them, and every block of that index's busiest expert is named by exactly 4.
All inputs are finite; a program needn't handle non-finite values.
Results may differ from the reference program's by a relative error of at most 0.023.
Values may be sent and summed in bfloat16 or wider, within the bound.
No kernel may reach another device: no remote copies, remote signals or barrier semaphores. Data moves between devices by JAX's collectives and lax.ppermute only.
A program may use at most 64 MiB of HBM per device.

```python
import jax
import jax.numpy as jnp
from jax import lax

D = 4608
BLOCK = 128
BLOCKS = 64
EXPERTS = 4
K = 4
TOK_DEV = 128
TOKENS = 16384
NB = 256
CAP = 4


def shared_routing(key):
    sources = TOKENS // TOK_DEV
    keys = jax.random.split(key, 5)
    hottest = jax.random.randint(keys[0], (sources,), 0, EXPERTS)
    orders = jax.vmap(lambda one_key: jax.random.permutation(one_key, TOK_DEV))(jax.random.split(keys[1], sources))
    is_hot = orders < TOK_DEV // 2
    offset = jax.random.randint(keys[2], (sources, TOK_DEV), 1, EXPERTS)
    expert = jnp.where(is_hot, hottest[:, None], (hottest[:, None] + offset) % EXPERTS).astype(jnp.int32)
    onehot = (expert[:, :, None] == jnp.arange(EXPERTS, dtype=jnp.int32)[None, None, :]).astype(jnp.int32)
    ranking = jnp.sum((jnp.cumsum(onehot, 1) - 1) * onehot, 2)
    starts = jax.random.randint(keys[3], (sources, EXPERTS), 0, BLOCKS)
    perms = jax.vmap(lambda one_key: jax.random.permutation(one_key, BLOCKS))(jax.random.split(keys[4], sources * EXPERTS))
    perms = perms.reshape(sources, EXPERTS, BLOCKS)
    base = jnp.take_along_axis(starts, expert, 1) + ranking * K
    position = (base[:, :, None] + jnp.arange(K, dtype=jnp.int32)[None, None, :]) % BLOCKS
    chosen = jnp.take_along_axis(perms, expert[:, :, None], 1)
    chosen = jnp.broadcast_to(chosen, (sources, TOK_DEV, BLOCKS))
    block_ids = jnp.take_along_axis(chosen, position, 2)
    return (expert.reshape(TOKENS).astype(jnp.int32), block_ids.reshape(TOKENS, K).astype(jnp.int32))


def draw_routes(key, part):
    expert, block_ids = shared_routing(key)
    return expert


def draw_blocks(key, part):
    expert, block_ids = shared_routing(key)
    return block_ids


def level_of(own_key, extent, pieces, least, high):
    def one(axis_at, blocks):
        draws = jax.random.uniform(jax.random.fold_in(jax.random.fold_in(own_key, 6), axis_at), (blocks,), jnp.float32, least / len(pieces), high / len(pieces))
        return jnp.repeat(jnp.exp(draws), extent[axis_at] // blocks).reshape((-1,) + (1,) * (len(extent) - axis_at - 1))

    level = one(*pieces[0])
    for cut in pieces[1:]:
        level = level * one(*cut)
    return level


def bell_draw(own_key, dims, width, limit, shards=(), kind=jnp.bfloat16):
    drawn = width * jax.random.normal(own_key, dims, jnp.float32)
    if shards:
        drawn = drawn * level_of(own_key, dims, shards, -0.22, 0.18)
    return jnp.clip(drawn, -limit, limit).astype(kind)


def setup_inputs(seed: int = 0) -> dict:
    key_of = jax.random.split(jax.random.key(seed), 8)
    residuals = bell_draw(key_of[0], (TOKENS, D), 1.0, 6.0, ((0, 128), (1, 4)))
    routes = draw_routes(jax.random.fold_in(key_of[7], 71), 0)
    blocks = draw_blocks(jax.random.fold_in(key_of[7], 71), 0)
    enc_weight = bell_draw(key_of[3], (NB, BLOCK, D), D ** -0.5, 0.09375, ((0, 128), (2, 4)))
    enc_bias = bell_draw(key_of[4], (NB, BLOCK), 0.5, 3.0, ((0, 128),), jnp.float32)
    dec_weight = bell_draw(key_of[5], (NB, BLOCK, D), (K * BLOCK) ** -0.5, 0.25, ((0, 128), (2, 4)))
    dec_bias = bell_draw(key_of[6], (D,), 0.5, 3.0, ((0, 4),), jnp.float32)
    return {"residuals": residuals, "routes": routes, "blocks": blocks, "enc_weight": enc_weight, "enc_bias": enc_bias, "dec_weight": dec_weight, "dec_bias": dec_bias}


L1_COEF = 0.2


def reference(residuals, routes, blocks, enc_weight, enc_bias, dec_weight, dec_bias):
    sources = TOKENS // TOK_DEV
    entries = TOK_DEV * K
    all_blocks = EXPERTS * BLOCKS
    global_block = (routes[:, None] * BLOCKS + blocks).reshape(sources, entries).astype(jnp.int32)
    onehot = (global_block[:, :, None] == jnp.arange(all_blocks, dtype=jnp.int32)[None, None, :]).astype(jnp.int32)
    ranking = jnp.sum((jnp.cumsum(onehot, 1) - 1) * onehot, 2).astype(jnp.int32)
    source_ids = jnp.arange(sources, dtype=jnp.int32)[:, None]
    table_row = ((global_block * sources + source_ids) * CAP + ranking).reshape(-1)
    entry_ids = jnp.arange(TOKENS * K, dtype=jnp.int32)
    table = jnp.full((all_blocks * sources * CAP,), TOKENS * K, jnp.int32).at[table_row].set(entry_ids)
    table = table.reshape(all_blocks, sources * CAP)
    valid = table < TOKENS * K
    token_ids = jnp.minimum(table // K, TOKENS - 1).astype(jnp.int32)

    def forward(carry, items):
        tok_index, present, enc_rows, bias_rows, dec_rows = items
        rows = jnp.where(present[:, None], residuals[tok_index], jnp.zeros((), jnp.bfloat16))
        pre = jnp.dot(rows, enc_rows.T, preferred_element_type=jnp.float32) + bias_rows[None, :]
        act = jax.nn.softplus(pre).astype(jnp.bfloat16)
        part = jnp.dot(act, dec_rows, preferred_element_type=jnp.float32).astype(jnp.bfloat16)
        added = jnp.where(present[:, None], part.astype(jnp.float32), jnp.zeros((), jnp.float32))
        carry = carry.at[tok_index].add(added)
        return carry, (pre, act)

    start = jnp.zeros((TOKENS, D), jnp.float32)
    summed, (pre_all, act_all) = lax.scan(forward, start, (token_ids, valid, enc_weight, enc_bias, dec_weight))
    recon = summed + dec_bias[None, :]
    reconstruction = recon.astype(jnp.bfloat16)
    error_rows = (recon - residuals.astype(jnp.float32)).astype(jnp.bfloat16)

    def backward(items):
        tok_index, present, enc_rows, dec_rows, pre, act = items
        rows = jnp.where(present[:, None], residuals[tok_index], jnp.zeros((), jnp.bfloat16))
        err_rows = jnp.where(present[:, None], error_rows[tok_index], jnp.zeros((), jnp.bfloat16))
        dec_g = jnp.dot(act.T, err_rows, preferred_element_type=jnp.float32).astype(jnp.bfloat16)
        dact = jnp.dot(err_rows, dec_rows.T, preferred_element_type=jnp.float32)
        slope = (dact + L1_COEF * present.astype(jnp.float32)[:, None]) * jax.nn.sigmoid(pre)
        enc_g = jnp.dot(slope.astype(jnp.bfloat16).T, rows, preferred_element_type=jnp.float32).astype(jnp.bfloat16)
        return enc_g, jnp.sum(slope, 0), dec_g

    enc_grad, enc_bias_grad, dec_grad = lax.map(backward, (token_ids, valid, enc_weight, dec_weight, pre_all, act_all))
    return reconstruction, enc_grad, enc_bias_grad, dec_grad
```

```python
import jax
import jax.numpy as jnp
from jax import lax
from jax.sharding import Mesh, PartitionSpec as P

BLOCKS = 64
L1_COEF = 0.2
CAP = 4
NY = 4
NZ = 16

F32 = jnp.float32
BF16 = jnp.bfloat16


def swap_cores(v):
    return lax.ppermute(v, "sect", [(0, 1), (1, 0)])


def y_ring(v, step):
    perm = [(y, (y + step) % NY) for y in range(NY)]
    perm += [(NY + y, NY + (y - step) % NY) for y in range(NY)]
    return lax.ppermute(v, ("sect", "y"), perm)


def gather_blocks(own):
    chip = jnp.stack([own, swap_cores(own)])
    near = y_ring(chip, 1)
    far = y_ring(near[0], 1)
    half = jnp.concatenate([own[None], near, far[None]])
    return jnp.concatenate([half, swap_cores(half)])


def scatter_blocks(part):
    half = part[:4].astype(F32) + swap_cores(part[4:]).astype(F32)
    half = half.astype(part.dtype)
    far = y_ring(half[3], -1)
    first = (half[1].astype(F32) + far.astype(F32)).astype(part.dtype)
    near = y_ring(jnp.stack([first, half[2]]), -1)
    return half[0].astype(F32) + near[0].astype(F32) + swap_cores(near[1]).astype(F32)


def peer_place(owner_sect, owner_y):
    sect, y = lax.axis_index("sect"), lax.axis_index("y")
    other = owner_sect ^ sect
    delta = owner_y - y
    delta = jnp.where(sect == 0, delta, -delta) & 3
    code = delta * 2 + other
    place = jnp.zeros_like(code)
    for at, value in enumerate((0, 4, 6, 5, 3, 7, 1, 2)):
        place = jnp.where(code == at, value, place)
    return place


def sum_lat(part):
    part = part.astype(BF16)
    turned = [
        lax.ppermute(part, "lat", [(i, (i + k) % 4) for i in range(4)]).astype(F32)
        for k in (1, 2, 3)
    ]
    return (part.astype(F32) + turned[1]) + (turned[0] + turned[2])


def shards(residuals, routes, blocks, enc_weight, enc_bias, dec_weight, dec_bias):
    tok_count, width = residuals.shape
    owned, latents, _ = enc_weight.shape
    local = 8 * owned
    pairs = NZ // 2
    z = lax.axis_index("z")

    rows = lax.all_gather(residuals, "z", axis=0, tiled=True).reshape(pairs, 2 * tok_count, width)

    weights = gather_blocks(jnp.stack([enc_weight, dec_weight]))
    enc_local = weights[:, 0].reshape(local, latents, width)
    dec_local = weights[:, 1].reshape(local, latents, width)
    bias_local = gather_blocks(enc_bias).reshape(local, latents)

    global_block = routes[:, None] * BLOCKS + blocks
    ids = lax.all_to_all(
        jnp.broadcast_to(global_block.reshape(1, -1), (NZ, tok_count * 4)), "z", 0, 0, tiled=True
    ).reshape(pairs, 2, tok_count, 4)
    place = peer_place(ids >> 7, (ids >> 5) & 3) * owned + (ids & 1)
    place = jnp.where(((ids >> 1) & 15) == z, place, -1)
    named = jnp.sum(
        (place[..., None] == jnp.arange(local, dtype=jnp.int32)).astype(F32), axis=3
    )
    lower = (
        jnp.arange(tok_count)[:, None] > jnp.arange(tok_count)[None, :]
    ).astype(BF16)
    rank = jnp.einsum("ut,pstk->psuk", lower, named.astype(BF16), preferred_element_type=F32)
    slot = rank + CAP * jnp.arange(2, dtype=F32)[None, :, None, None]
    slot = jnp.where(named > 0, slot, -1.0).reshape(pairs, 2 * tok_count, local)
    slot = slot.transpose(0, 2, 1)
    pick = (
        slot[:, :, None, :] == jnp.arange(2 * CAP, dtype=F32)[None, None, :, None]
    ).astype(BF16)
    present = jnp.sum(pick.astype(F32), axis=3).transpose(1, 0, 2).reshape(local, -1)

    def to_slots(v):
        taken = jnp.einsum("pkrt,ptd->kprd", pick, v, preferred_element_type=F32).astype(BF16)
        return taken.reshape(local, pairs * 2 * CAP, width)

    incoming = to_slots(rows)
    pre_part = jnp.einsum("krd,kld->krl", incoming, enc_local, preferred_element_type=F32)
    pre = sum_lat(pre_part) + bias_local[:, None, :]
    act = jax.nn.softplus(pre).astype(BF16)
    part = jnp.einsum("krl,kld->krd", act, dec_local, preferred_element_type=F32).astype(BF16)
    part = part.reshape(local, pairs, 2 * CAP, width)
    home = jnp.einsum("pkrt,kprd->ptd", pick, part, preferred_element_type=F32).astype(BF16)
    total = lax.psum_scatter(
        home.reshape(NZ * tok_count, width), "z", scatter_dimension=0, tiled=True
    )
    recon = total.astype(F32) + dec_bias[None, :]
    reconstruction = recon.astype(BF16)
    error = (recon - residuals.astype(F32)).astype(BF16)
    errors = lax.all_gather(error, "z", axis=0, tiled=True).reshape(pairs, 2 * tok_count, width)
    error_in = to_slots(errors)
    dact_part = jnp.einsum("krd,kld->krl", error_in, dec_local, preferred_element_type=F32)
    dact = sum_lat(dact_part)
    dec_part = jnp.einsum("krl,krd->kld", act, error_in, preferred_element_type=F32).astype(BF16)
    dec_grad = scatter_blocks(dec_part.reshape(8, owned, latents, width)).astype(BF16)
    slope = (dact + L1_COEF * present[..., None]) * jax.nn.sigmoid(pre)
    enc_part = jnp.einsum(
        "krl,krd->kld", slope.astype(BF16), incoming, preferred_element_type=F32
    ).astype(BF16)
    enc_grad = scatter_blocks(enc_part.reshape(8, owned, latents, width)).astype(BF16)
    enc_bias_grad = scatter_blocks(jnp.sum(slope, 1).reshape(8, owned, latents))
    return reconstruction, enc_grad, enc_bias_grad, dec_grad


def solution(mesh):
    fine = Mesh(mesh.devices.reshape(2, NY, NZ, 4), ("sect", "y", "z", "lat"))
    own = ("sect", "y", "z")
    return jax.shard_map(
        shards,
        mesh=fine,
        in_specs=(
            P(own, "lat"),
            P(own),
            P(own, None),
            P(own, None, "lat"),
            P(own, None),
            P(own, None, "lat"),
            P("lat"),
        ),
        out_specs=(
            P(own, "lat"),
            P(own, None, "lat"),
            P(own, None),
            P(own, None, "lat"),
        ),
        check_vma=False,
    )
```

```python
import jax
import jax.numpy as jnp
from jax import lax
from jax.sharding import Mesh, PartitionSpec as P

BLOCKS = 64
L1_COEF = 0.2
CAP = 4
NY = 4
NZ = 16

F32 = jnp.float32
BF16 = jnp.bfloat16


def swap_cores(v):
    return lax.ppermute(v, "sect", [(0, 1), (1, 0)])


def y_ring(v, step):
    perm = [(y, (y + step) % NY) for y in range(NY)]
    perm += [(NY + y, NY + (y - step) % NY) for y in range(NY)]
    return lax.ppermute(v, ("sect", "y"), perm)


def gather_blocks(own):
    chip = jnp.stack([own, swap_cores(own)])
    near = y_ring(chip, 1)
    far = y_ring(near[0], 1)
    half = jnp.concatenate([own[None], near, far[None]])
    return half, swap_cores(half)


def scatter_blocks(half, other):
    other = swap_cores(other)
    away = y_ring((half[2:].astype(F32) + other[2:].astype(F32)).astype(half.dtype), -1)
    near = half[1].astype(F32) + other[1].astype(F32) + away[1].astype(F32)
    near = y_ring(near.astype(half.dtype), -1)
    own = half[0].astype(F32) + other[0].astype(F32) + swap_cores(away[0]).astype(F32)
    return own + near.astype(F32)


def peer_place(owner_sect, owner_y):
    sect, y = lax.axis_index("sect"), lax.axis_index("y")
    other = owner_sect ^ sect
    delta = owner_y - y
    delta = jnp.where(sect == 0, delta, -delta) & 3
    code = delta * 2 + other
    place = jnp.zeros_like(code)
    for at, value in enumerate((0, 4, 6, 5, 3, 7, 1, 2)):
        place = jnp.where(code == at, value, place)
    return place


def sum_lat(part):
    part = part.astype(BF16)
    copies = lax.all_to_all(jnp.broadcast_to(part[None], (4,) + part.shape), "lat", 0, 0)
    return jnp.sum(copies.astype(F32), 0)


def routing(place, local):
    sources, _, toks = place.shape
    named = jnp.sum(
        (place[:, :, None, :] == jnp.arange(local, dtype=jnp.int32)[None, None, :, None]).astype(F32), 1
    )
    before = (jnp.arange(toks)[:, None] < jnp.arange(toks)[None, :]).astype(BF16)
    rank = jnp.einsum("skt,tu->sku", named.astype(BF16), before, preferred_element_type=F32)
    slot = rank + CAP * (jnp.arange(sources, dtype=jnp.int32) % 2).astype(F32)[:, None, None]
    slot = jnp.where(named > 0, slot, -1.0)
    slot = slot.reshape(sources // 2, 2, local, toks).transpose(0, 2, 1, 3)
    slot = slot.reshape(sources // 2, local, 2 * toks)
    return (
        slot[:, :, None, :] == jnp.arange(2 * CAP, dtype=F32)[None, None, :, None]
    ).astype(BF16)


def to_slots(pick, v):
    taken = jnp.einsum("pkrt,ptd->kprd", pick, v, preferred_element_type=F32).astype(BF16)
    return taken.reshape(taken.shape[0], -1, taken.shape[3])


def shards(residuals, routes, blocks, enc_weight, enc_bias, dec_weight, dec_bias):
    tok_count, width = residuals.shape
    owned, latents, _ = enc_weight.shape
    local = 8 * owned
    half = local // 2
    pairs = NZ // 2
    sect, y, z = lax.axis_index("sect"), lax.axis_index("y"), lax.axis_index("z")

    def local_blocks(w):
        return [h.reshape(half, *w.shape[1:]) for h in gather_blocks(w)]

    rows = lax.all_gather(residuals, "z", axis=0, tiled=True).reshape(pairs, 2 * tok_count, width)

    global_block = (routes[:, None] * BLOCKS + blocks).T.reshape(1, 4, tok_count)
    ids = lax.all_to_all(
        jnp.broadcast_to(global_block, (NZ, 4, tok_count)), "z", 0, 0, tiled=True
    )
    bias_local = jnp.concatenate(local_blocks(enc_bias))
    ids, bias_local = lax.optimization_barrier((ids, bias_local))
    here = ((ids >> 1) & 15) == z
    place = jnp.where(here, peer_place(ids >> 7, (ids >> 5) & 3) * owned + (ids & 1), -1)
    pick = routing(place, local)
    present = jnp.sum(pick.astype(F32), axis=3).transpose(1, 0, 2).reshape(local, -1)

    enc_local = local_blocks(enc_weight)
    dec_local = local_blocks(dec_weight)

    def halves(v):
        return [to_slots(pick[:, :half], v), to_slots(pick[:, half:], v)]

    def into_latents(v, w):
        return jnp.concatenate(
            [
                jnp.einsum("krd,kld->krl", a, b, preferred_element_type=F32).astype(BF16)
                for a, b in zip(v, w)
            ]
        )

    pre = sum_lat(into_latents(halves(rows), enc_local)) + bias_local[:, None, :]
    act = jax.nn.softplus(pre).astype(BF16)
    act_halves = [act[:half], act[half:]]
    part = [
        jnp.einsum("krl,kld->krd", a, b, preferred_element_type=F32).astype(BF16)
        for a, b in zip(act_halves, dec_local)
    ]
    part = jnp.concatenate(part).reshape(local, pairs, 2 * CAP, width)
    home = jnp.einsum("pkrt,kprd->ptd", pick, part, preferred_element_type=F32).astype(BF16)
    home, rows, ids = lax.optimization_barrier((home, rows, ids))
    total = lax.psum_scatter(
        home.reshape(NZ * tok_count, width), "z", scatter_dimension=0, tiled=True
    )

    here = ((ids >> 1) & 15) == z
    straight = routing(jnp.where(here, (ids >> 5) * owned + (ids & 1), -1), local)
    owner_rows = lax.all_to_all(
        to_slots(straight, rows).reshape(8, owned, -1, width), ("sect", "y"), 0, 0, tiled=True
    )
    owner_rows = owner_rows.transpose(1, 0, 2, 3).reshape(owned, -1, width)

    total, owner_rows = lax.optimization_barrier((total, owner_rows))
    recon = total.astype(F32) + dec_bias[None, :]
    reconstruction = recon.astype(BF16)
    error = (recon - residuals.astype(F32)).astype(BF16)
    errors = lax.all_gather(error, "z", axis=0, tiled=True).reshape(pairs, 2 * tok_count, width)
    error_in = halves(errors)
    dact = into_latents(error_in, dec_local)
    error_in, dact = lax.optimization_barrier((error_in, dact))
    dact = sum_lat(dact)
    dec_part = [
        jnp.einsum("krl,krd->kld", a, b, preferred_element_type=F32)
        .astype(BF16)
        .reshape(4, owned, latents, width)
        for a, b in zip(act_halves, error_in)
    ]
    dec_grad = scatter_blocks(*dec_part).astype(BF16)
    slope = ((dact + L1_COEF * present[..., None]) * jax.nn.sigmoid(pre)).astype(BF16)
    peers = jnp.arange(8, dtype=jnp.int32)
    order = (peer_place(peers >> 2, peers & 3)[:, None] == peers[None, :]).astype(BF16)
    slope = jnp.einsum(
        "ap,pm->am", order, slope.reshape(8, -1), preferred_element_type=F32
    ).astype(BF16)
    owner_slope = lax.all_to_all(
        slope.reshape(8, owned, -1, latents), ("sect", "y"), 0, 0, tiled=True
    )
    owner_slope = owner_slope.transpose(1, 0, 2, 3).reshape(owned, -1, latents)
    enc_bias_grad = jnp.sum(owner_slope.astype(F32), 1)
    enc_grad = jnp.einsum(
        "brl,brd->bld", owner_slope, owner_rows, preferred_element_type=F32
    ).astype(BF16)
    return reconstruction, enc_grad, enc_bias_grad, dec_grad


def solution(mesh):
    fine = Mesh(mesh.devices.reshape(2, NY, NZ, 4), ("sect", "y", "z", "lat"))
    own = ("sect", "y", "z")
    return jax.shard_map(
        shards,
        mesh=fine,
        in_specs=(
            P(own, "lat"),
            P(own),
            P(own, None),
            P(own, None, "lat"),
            P(own, None),
            P(own, None, "lat"),
            P("lat"),
        ),
        out_specs=(
            P(own, "lat"),
            P(own, None, "lat"),
            P(own, None),
            P(own, None, "lat"),
        ),
        check_vma=False,
    )
```

```python
import jax
import jax.numpy as jnp
from jax import lax
from jax.experimental import pallas as pl
from jax.experimental.pallas import tpu as pltpu
from jax.sharding import Mesh, PartitionSpec as P

BLOCKS = 64
L1_COEF = 0.2
CAP = 4
NY = 4
NZ = 16
GROUP = 4
TILES = 3

F32 = jnp.float32
BF16 = jnp.bfloat16


def swap_cores(v):
    return lax.ppermute(v, "sect", [(0, 1), (1, 0)])


def y_ring(v, step):
    perm = [(y, (y + step) % NY) for y in range(NY)]
    perm += [(NY + y, NY + (y - step) % NY) for y in range(NY)]
    return lax.ppermute(v, ("sect", "y"), perm)


def add_body(*refs):
    *values, out = refs
    total = values[0][...].astype(F32)
    for v in values[1:]:
        total = total + v[...].astype(F32)
    out[...] = total.astype(out.dtype)


def add(*terms, count=1):
    first = terms[0][0]
    shape = (1, 1) + first.shape[2:]
    rest = (0,) * (first.ndim - 2)
    return pl.pallas_call(
        add_body,
        grid=(count, first.shape[1]),
        in_specs=[
            pl.BlockSpec(shape, lambda i, j, at=at: (i + at, j) + rest) for _, at in terms
        ],
        out_specs=pl.BlockSpec(shape, lambda i, j: (i, j) + rest),
        out_shape=jax.ShapeDtypeStruct((count,) + first.shape[1:], first.dtype),
        cost_estimate=pl.CostEstimate(flops=0, bytes_accessed=3_000_000, transcendentals=0),
    )(*[v for v, _ in terms])


def gather_blocks(own):
    chip = jnp.stack([own, swap_cores(own)])
    near = y_ring(chip, 1)
    far = y_ring(near[0], 1)
    half = jnp.concatenate([own[None], near, far[None]])
    return half, swap_cores(half)


def scatter_blocks(half, other):
    other = swap_cores(other)
    away = y_ring(add((half, 2), (other, 2), count=2), -1)
    near = y_ring(add((half, 1), (other, 1), (away, 1)), -1)
    side = swap_cores(away[:1])
    return add((half, 0), (other, 0), (side, 0), (near, 0))[0]


def peer_place(owner_sect, owner_y):
    sect, y = lax.axis_index("sect"), lax.axis_index("y")
    other = owner_sect ^ sect
    delta = owner_y - y
    delta = jnp.where(sect == 0, delta, -delta) & 3
    code = delta * 2 + other
    place = jnp.zeros_like(code)
    for at, value in enumerate((0, 4, 6, 5, 3, 7, 1, 2)):
        place = jnp.where(code == at, value, place)
    return place


def routing(place, local):
    sources, _, toks = place.shape
    groups = sources // GROUP
    named = jnp.sum(
        (place[:, :, None, :] == jnp.arange(local, dtype=jnp.int32)[None, None, :, None]).astype(F32), 1
    )
    before = (jnp.arange(toks)[:, None] < jnp.arange(toks)[None, :]).astype(BF16)
    rank = jnp.einsum("skt,tu->sku", named.astype(BF16), before, preferred_element_type=F32)
    slot = rank + CAP * (jnp.arange(sources, dtype=jnp.int32) % GROUP).astype(F32)[:, None, None]
    slot = jnp.where(named > 0, slot, -1.0)
    slot = slot.reshape(groups, GROUP, local, toks).transpose(0, 2, 1, 3)
    slot = slot.reshape(groups, local, GROUP * toks)
    return (
        slot[:, :, None, :] == jnp.arange(GROUP * CAP, dtype=F32)[None, None, :, None]
    ).astype(BF16)


def to_slots(pick, v):
    taken = jnp.einsum("pkrt,ptd->kprd", pick, v, preferred_element_type=F32).astype(BF16)
    return taken.reshape(taken.shape[0], -1, taken.shape[3])


def whole(*shape):
    return pl.BlockSpec(shape, lambda i: (0,) * len(shape))


def columns(*shape):
    return pl.BlockSpec(shape, lambda i: (0,) * (len(shape) - 1) + (i,))


PARAMS = pltpu.CompilerParams(
    dimension_semantics=("arbitrary",), vmem_limit_bytes=40 * 1024 * 1024
)


def project_body(grads, *refs):
    if grads:
        pick, rows, wa, wb, act, out, ga, gb, slots, total = refs
    else:
        pick, rows, wa, wb, out, slots, total = refs
    step = pl.program_id(0)

    @pl.when(step == 0)
    def _():
        total[...] = jnp.zeros_like(total)

    groups, wide, _ = pick.shape
    local = slots.shape[0]
    each = wide // local
    for q in range(groups):
        taken = jnp.dot(pick[q], rows[q], preferred_element_type=F32).astype(BF16)
        slots[:, q * each : (q + 1) * each, :] = taken.reshape(local, each, taken.shape[1])
    for k in range(local):
        w = wa[k] if k < local // 2 else wb[k - local // 2]
        part = jnp.dot(slots[k], w, preferred_element_type=F32)
        total[k] = total[k] + part
        if grads:
            g = jnp.dot(act[k], slots[k], preferred_element_type=F32).astype(BF16)
            if k < local // 2:
                ga[k] = g
            else:
                gb[k - local // 2] = g

    @pl.when(step == TILES - 1)
    def _():
        value = total[...].astype(BF16)
        for c in range(out.shape[0]):
            out[c] = value


def project(pick, rows, wa, wb, act=None):
    groups, wide, toks = pick.shape
    half, width, latents = wa.shape
    local, tile = 2 * half, width // TILES
    count = groups * wide // local
    depth = pl.BlockSpec((half, tile, latents), lambda i: (0, i, 0))
    ins = [pick, rows, wa, wb]
    in_specs = [
        whole(groups, wide, toks),
        columns(groups, toks, tile),
        depth,
        depth,
    ]
    outs = [jax.ShapeDtypeStruct((4, local, count, latents), BF16)]
    out_specs = [whole(4, local, count, latents)]
    if act is not None:
        ins.append(act)
        in_specs.append(whole(local, latents, count))
        outs += [jax.ShapeDtypeStruct((half, latents, width), BF16)] * 2
        out_specs += [columns(half, latents, tile)] * 2
    return pl.pallas_call(
        lambda *refs: project_body(act is not None, *refs),
        grid=(TILES,),
        in_specs=in_specs,
        out_specs=out_specs,
        out_shape=outs,
        scratch_shapes=[
            pltpu.VMEM((local, count, tile), BF16),
            pltpu.VMEM((local, count, latents), F32),
        ],
        compiler_params=PARAMS,
        cost_estimate=pl.CostEstimate(
            flops=2 * groups * wide * toks * width, bytes_accessed=12_000_000, transcendentals=0
        ),
    )(*ins)


def decode_body(copies, bias, turned, wa, wb, pre, act, home, part):
    step = pl.program_id(0)
    groups, _, wide = turned.shape
    local = part.shape[0]
    each = wide // local

    @pl.when(step == 0)
    def _():
        value = copies[0].astype(F32)
        for c in range(1, copies.shape[0]):
            value = value + copies[c].astype(F32)
        value = value + bias[...][:, None, :]
        pre[...] = value
        soft = jnp.maximum(value, 0.0) + jnp.log1p(jnp.exp(-jnp.abs(value)))
        act[...] = soft.astype(BF16)

    for k in range(local):
        w = wa[k] if k < local // 2 else wb[k - local // 2]
        part[k] = jnp.dot(act[k], w, preferred_element_type=F32).astype(BF16)
    for q in range(groups):
        rows = part[:, q * each : (q + 1) * each, :].reshape(wide, part.shape[2])
        home[q] = jnp.dot(turned[q], rows, preferred_element_type=F32).astype(BF16)


def decode(copies, bias, turned, wa, wb):
    groups, toks, wide = turned.shape
    half, latents, width = wa.shape
    local, tile = 2 * half, width // TILES
    count = groups * wide // local
    return pl.pallas_call(
        decode_body,
        grid=(TILES,),
        in_specs=[
            whole(4, local, count, latents),
            whole(local, latents),
            whole(groups, toks, wide),
            columns(half, latents, tile),
            columns(half, latents, tile),
        ],
        out_specs=[
            whole(local, count, latents),
            whole(local, count, latents),
            columns(groups, toks, tile),
        ],
        out_shape=[
            jax.ShapeDtypeStruct((local, count, latents), F32),
            jax.ShapeDtypeStruct((local, count, latents), BF16),
            jax.ShapeDtypeStruct((groups, toks, width), BF16),
        ],
        scratch_shapes=[pltpu.VMEM((local, count, tile), BF16)],
        compiler_params=PARAMS,
        cost_estimate=pl.CostEstimate(
            flops=2 * groups * wide * toks * width, bytes_accessed=12_000_000, transcendentals=0
        ),
    )(copies, bias, turned, wa, wb)


def slope_body(order, copies, flat, sig, out):
    owned = out.shape[1]
    for a in range(out.shape[0]):
        for i in range(owned):
            k = order[a] * owned + i
            value = copies[0, k].astype(F32)
            for c in range(1, copies.shape[0]):
                value = value + copies[c, k].astype(F32)
            out[a, i] = ((value + flat[k]) * sig[k]).astype(BF16)


def slopes(order, copies, flat, sig):
    _, local, count, latents = copies.shape
    return pl.pallas_call(
        slope_body,
        in_specs=[pl.BlockSpec(memory_space=pltpu.SMEM)]
        + [pl.BlockSpec(memory_space=pltpu.VMEM)] * 3,
        out_specs=pl.BlockSpec(memory_space=pltpu.VMEM),
        out_shape=jax.ShapeDtypeStruct((8, local // 8, count, latents), BF16),
        cost_estimate=pl.CostEstimate(flops=0, bytes_accessed=2_500_000, transcendentals=0),
    )(order, copies, flat, sig)


def over_lat(copies):
    return lax.all_to_all(copies, "lat", 0, 0, tiled=True)


def shards(residuals, routes, blocks, enc_weight, enc_bias, dec_weight, dec_bias):
    tok_count, width = residuals.shape
    owned, latents, _ = enc_weight.shape
    local = 8 * owned
    half = local // 2
    groups = NZ // GROUP
    sect, y, z = lax.axis_index("sect"), lax.axis_index("y"), lax.axis_index("z")

    def local_blocks(w):
        return [h.reshape(half, *w.shape[1:]) for h in gather_blocks(w)]

    rows = lax.all_gather(residuals, "z", axis=0, tiled=True).reshape(groups, GROUP * tok_count, width)

    global_block = (routes[:, None] * BLOCKS + blocks).T.reshape(1, 4, tok_count)
    ids = lax.all_to_all(
        jnp.broadcast_to(global_block, (NZ, 4, tok_count)), "z", 0, 0, tiled=True
    )
    bias_local = jnp.concatenate(local_blocks(enc_bias))
    ids, bias_local = lax.optimization_barrier((ids, bias_local))
    here = ((ids >> 1) & 15) == z
    place = jnp.where(here, peer_place(ids >> 7, (ids >> 5) & 3) * owned + (ids & 1), -1)
    pick = routing(place, local)
    present = jnp.sum(pick.astype(F32), axis=3).transpose(1, 0, 2).reshape(local, -1)
    pick = pick.reshape(groups, -1, GROUP * tok_count)
    turned = pick.transpose(0, 2, 1)

    enc_local = local_blocks(enc_weight)
    dec_local = local_blocks(dec_weight)

    pre_part, = project(pick, rows, *[w.swapaxes(1, 2) for w in enc_local])
    pre, act, home = decode(over_lat(pre_part), bias_local, turned, *dec_local)
    home, rows, ids = lax.optimization_barrier((home, rows, ids))
    total = lax.psum_scatter(
        home.reshape(NZ * tok_count, width), "z", scatter_dimension=0, tiled=True
    )

    here = ((ids >> 1) & 15) == z
    straight = routing(jnp.where(here, (ids >> 5) * owned + (ids & 1), -1), local)
    owner_rows = lax.all_to_all(
        to_slots(straight, rows).reshape(8, owned, -1, width), ("sect", "y"), 0, 0, tiled=True
    )
    owner_rows = owner_rows.transpose(1, 0, 2, 3).reshape(owned, -1, width)

    turned_dec = [w.swapaxes(1, 2) for w in dec_local]
    turned_act = act.swapaxes(1, 2)
    flat = jnp.broadcast_to(L1_COEF * present[..., None], pre.shape)
    sig = jax.nn.sigmoid(pre)
    peers = jnp.arange(8, dtype=jnp.int32)
    order = peer_place(peers >> 2, peers & 3)
    total, owner_rows, turned_dec, turned_act, flat, sig, order = lax.optimization_barrier(
        (total, owner_rows, turned_dec, turned_act, flat, sig, order)
    )
    recon = total.astype(F32) + dec_bias[None, :]
    reconstruction = recon.astype(BF16)
    error = (recon - residuals.astype(F32)).astype(BF16)
    errors = lax.all_gather(error, "z", axis=0, tiled=True).reshape(groups, GROUP * tok_count, width)
    dact, *dec_part = project(pick, errors, *turned_dec, turned_act)
    owner_slope = lax.all_to_all(
        slopes(order, over_lat(dact), flat, sig), ("sect", "y"), 0, 0, tiled=True
    )
    dec_grad = scatter_blocks(*[g.reshape(4, owned, latents, width) for g in dec_part])
    owner_slope = owner_slope.transpose(1, 0, 2, 3).reshape(owned, -1, latents)
    enc_bias_grad = jnp.sum(owner_slope.astype(F32), 1)
    enc_grad = jnp.einsum(
        "brl,brd->bld", owner_slope, owner_rows, preferred_element_type=F32
    ).astype(BF16)
    return reconstruction, enc_grad, enc_bias_grad, dec_grad


def solution(mesh):
    fine = Mesh(mesh.devices.reshape(2, NY, NZ, 4), ("sect", "y", "z", "lat"))
    own = ("sect", "y", "z")
    return jax.shard_map(
        shards,
        mesh=fine,
        in_specs=(
            P(own, "lat"),
            P(own),
            P(own, None),
            P(own, None, "lat"),
            P(own, None),
            P(own, None, "lat"),
            P("lat"),
        ),
        out_specs=(
            P(own, "lat"),
            P(own, None, "lat"),
            P(own, None),
            P(own, None, "lat"),
        ),
        check_vma=False,
    )
```

```python
import jax
import jax.numpy as jnp
from jax import lax
from jax.experimental import pallas as pl
from jax.experimental.pallas import tpu as pltpu
from jax.sharding import Mesh, PartitionSpec as P

BLOCKS = 64
L1_COEF = 0.2
CAP = 4
NY = 4
NZ = 16
GROUP = 4
TILES = 3
LOCAL = 16

F32 = jnp.float32
BF16 = jnp.bfloat16


def swap_cores(v):
    return lax.ppermute(v, "sect", [(0, 1), (1, 0)])


def y_ring(v, step):
    perm = [(y, (y + step) % NY) for y in range(NY)]
    perm += [(NY + y, NY + (y - step) % NY) for y in range(NY)]
    return lax.ppermute(v, ("sect", "y"), perm)


def gather_half(own):
    chip = jnp.stack([own, swap_cores(own)])
    near = y_ring(chip, 1)
    far = y_ring(near[0], 1)
    return jnp.concatenate([own[None], near, far[None]])


def tie(*values):
    return lax.optimization_barrier(values)


def peer_place(owner_sect, owner_y):
    sect, y = lax.axis_index("sect"), lax.axis_index("y")
    other = owner_sect ^ sect
    delta = owner_y - y
    delta = jnp.where(sect == 0, delta, -delta) & 3
    code = delta * 2 + other
    place = jnp.zeros_like(code)
    for at, value in enumerate((0, 4, 6, 5, 3, 7, 1, 2)):
        place = jnp.where(code == at, value, place)
    return place


def routing(place, local):
    sources, _, toks = place.shape
    groups = sources // GROUP
    named = jnp.sum(
        (place[:, :, None, :] == jnp.arange(local, dtype=jnp.int32)[None, None, :, None]).astype(F32), 1
    )
    before = (jnp.arange(toks)[:, None] < jnp.arange(toks)[None, :]).astype(BF16)
    rank = jnp.einsum("skt,tu->sku", named.astype(BF16), before, preferred_element_type=F32)
    slot = rank + CAP * (jnp.arange(sources, dtype=jnp.int32) % GROUP).astype(F32)[:, None, None]
    slot = jnp.where(named > 0, slot, -1.0)
    slot = slot.reshape(groups, GROUP, local, toks).transpose(0, 2, 1, 3)
    slot = slot.reshape(groups, local, GROUP * toks)
    number = jnp.arange(GROUP * CAP, dtype=F32)
    pick = (slot[:, :, None, :] == number[None, None, :, None]).astype(BF16)
    turned = jnp.repeat(slot.transpose(0, 2, 1), GROUP * CAP, axis=2)
    turned = (turned == jnp.tile(number, local)[None, None, :]).astype(BF16)
    return pick.reshape(groups, -1, GROUP * toks), turned


def whole(*shape):
    return pl.BlockSpec(shape, lambda i: (0,) * len(shape))


def columns(*shape):
    return pl.BlockSpec(shape, lambda i: (0,) * (len(shape) - 1) + (i,))


PARAMS = pltpu.CompilerParams(
    dimension_semantics=("arbitrary",), vmem_limit_bytes=58 * 1024 * 1024
)


def take(pick, rows, slots):
    groups, wide, _ = pick.shape
    each = wide // LOCAL
    for q in range(groups):
        taken = jnp.dot(pick[q], rows[q], preferred_element_type=F32).astype(BF16)
        slots[:, q * each : (q + 1) * each, :] = taken.reshape(LOCAL, each, taken.shape[1])


def placed(order, wa, wb, k, owned):
    place = order[k // owned]
    at = (place & 3) * owned + k % owned
    return jnp.where(place < 4, wa[at], wb[at])


ORDER = pl.BlockSpec(memory_space=pltpu.SMEM)


def call(body, ins, in_specs, outs, out_specs, scratch, flops, moved):
    return pl.pallas_call(
        body,
        grid=(TILES,),
        in_specs=in_specs,
        out_specs=out_specs,
        out_shape=[jax.ShapeDtypeStruct(shape, kind) for shape, kind in outs],
        scratch_shapes=scratch,
        compiler_params=PARAMS,
        cost_estimate=pl.CostEstimate(flops=flops, bytes_accessed=moved, transcendentals=0),
    )(*ins)


def select(pick, rows):
    groups, wide, toks = pick.shape
    width = rows.shape[2]
    count = groups * wide // LOCAL
    return call(
        take,
        (pick, rows),
        [whole(groups, wide, toks), columns(groups, toks, width // TILES)],
        [((LOCAL, count, width), BF16)],
        [columns(LOCAL, count, width // TILES)],
        [],
        2 * groups * wide * toks * width,
        8_000_000,
    )[0]


def project_body(order, pick, rows, wa, wb, out, slots, total):
    step = pl.program_id(0)

    @pl.when(step == 0)
    def _():
        total[...] = jnp.zeros_like(total)

    take(pick, rows, slots)
    for k in range(LOCAL):
        w = placed(order, wa, wb, k, LOCAL // 8)
        total[k] = total[k] + jnp.dot(slots[k], w, preferred_element_type=F32)

    @pl.when(step == TILES - 1)
    def _():
        out[...] = total[...].astype(BF16)


def project(order, pick, rows, wa, wb, keep):
    groups, wide, toks = pick.shape
    half, _, latents = wa.shape
    width = rows.shape[2]
    tile = width // TILES
    count = groups * wide // LOCAL
    depth = pl.BlockSpec((half, tile, latents), lambda i: (0, i, 0))
    outs = [((LOCAL, count, latents), BF16)]
    out_specs = [whole(LOCAL, count, latents)]
    scratch = [pltpu.VMEM((LOCAL, count, latents), F32)]
    if keep:
        outs.append(((LOCAL, count, width), BF16))
        out_specs.append(columns(LOCAL, count, tile))
    else:
        scratch.insert(0, pltpu.VMEM((LOCAL, count, tile), BF16))
    return call(
        project_body,
        (order, pick, rows, wa, wb),
        [ORDER, whole(groups, wide, toks), columns(groups, toks, tile), depth, depth],
        outs,
        out_specs,
        scratch,
        2 * groups * wide * toks * width,
        12_000_000,
    )


def over_lat(part):
    return [part] + [
        lax.ppermute(part, "lat", [(i, (i + k) % 4) for i in range(4)]) for k in (1, 2, 3)
    ]


def sum_lat(a, b, c, d):
    return (a.astype(F32) + c.astype(F32)) + (b.astype(F32) + d.astype(F32))


def decode_body(order, a, b, c, d, bias, turned, wa, wb, pre, act, home, part):
    groups, _, wide = turned.shape
    each = wide // LOCAL

    @pl.when(pl.program_id(0) == 0)
    def _():
        for k in range(LOCAL):
            owned = LOCAL // 8
            at = order[k // owned] * owned + k % owned
            value = sum_lat(a[k], b[k], c[k], d[k]) + bias[at]
            pre[k] = value
            soft = jnp.maximum(value, 0.0) + jnp.log1p(jnp.exp(-jnp.abs(value)))
            act[k] = soft.astype(BF16)

    for k in range(LOCAL):
        w = placed(order, wa, wb, k, LOCAL // 8)
        part[k] = jnp.dot(act[k], w, preferred_element_type=F32).astype(BF16)
    for q in range(groups):
        rows = part[:, q * each : (q + 1) * each, :].reshape(wide, part.shape[2])
        home[q] = jnp.dot(turned[q], rows, preferred_element_type=F32).astype(BF16)


def decode(order, part, bias, turned, wa, wb):
    groups, toks, wide = turned.shape
    half, latents, width = wa.shape
    tile = width // TILES
    count = groups * wide // LOCAL
    return call(
        decode_body,
        (order, *over_lat(part), bias, turned, wa, wb),
        [
            ORDER,
            *[whole(LOCAL, count, latents)] * 4,
            whole(LOCAL, 1, latents),
            whole(groups, toks, wide),
            columns(half, latents, tile),
            columns(half, latents, tile),
        ],
        [
            ((LOCAL, count, latents), F32),
            ((LOCAL, count, latents), BF16),
            ((groups, toks, width), BF16),
        ],
        [
            whole(LOCAL, count, latents),
            whole(LOCAL, count, latents),
            columns(groups, toks, tile),
        ],
        [pltpu.VMEM((LOCAL, count, tile), BF16)],
        2 * groups * wide * toks * width,
        12_000_000,
    )


def slope_body(a, b, c, d, sig, out):
    out[...] = ((sum_lat(a[...], b[...], c[...], d[...]) + L1_COEF) * sig[...]).astype(BF16)


def slopes(part, sig):
    return pl.pallas_call(
        slope_body,
        in_specs=[pl.BlockSpec(memory_space=pltpu.VMEM)] * 5,
        out_specs=pl.BlockSpec(memory_space=pltpu.VMEM),
        out_shape=jax.ShapeDtypeStruct(sig.shape, BF16),
        compiler_params=pltpu.CompilerParams(vmem_limit_bytes=16 * 1024 * 1024),
        cost_estimate=pl.CostEstimate(flops=0, bytes_accessed=2_500_000, transcendentals=0),
    )(*over_lat(part), sig)


def outer_body(values, rows, grad, sums, turned):
    peers, owned, count, tile = rows.shape

    @pl.when(pl.program_id(0) == 0)
    def _():
        for i in range(owned):
            value = values[:, i].reshape(peers * count, values.shape[3]).astype(F32)
            sums[i, :] = jnp.sum(value, 0)
            turned[i] = value.T.astype(BF16)

    for i in range(owned):
        grad[i] = jnp.dot(
            turned[i], rows[:, i].reshape(peers * count, tile), preferred_element_type=F32
        ).astype(BF16)


def outer(values, rows):
    peers, owned, count, width = rows.shape
    latents = values.shape[3]
    tile = width // TILES
    return call(
        outer_body,
        (values, rows),
        [whole(peers, owned, count, latents), columns(peers, owned, count, tile)],
        [((owned, latents, width), BF16), ((owned, latents), F32)],
        [columns(owned, latents, tile), whole(owned, latents)],
        [pltpu.VMEM((owned, latents, peers * count), BF16)],
        4 * peers * count * width * latents,
        5_000_000,
    )


def shards(residuals, routes, blocks, enc_weight, enc_bias, dec_weight, dec_bias):
    tok_count, width = residuals.shape
    owned, latents, _ = enc_weight.shape
    half = LOCAL // 2
    groups = NZ // GROUP
    z = lax.axis_index("z")

    def both(part):
        return [h.reshape(half, *h.shape[2:]) for h in (part, swap_cores(part))]

    def to_owners(v):
        return lax.all_to_all(
            v.reshape(8, owned, *v.shape[1:]), ("sect", "y"), 0, 0, tiled=True
        )

    def over_z(v):
        v = lax.all_gather(v, "z", axis=0, tiled=True)
        return v.reshape(groups, GROUP * tok_count, width)

    rows = over_z(residuals)

    global_block = (routes[:, None] * BLOCKS + blocks).T.reshape(1, 4, tok_count)
    ids = lax.all_to_all(
        jnp.broadcast_to(global_block, (NZ, 4, tok_count)), "z", 0, 0, tiled=True
    )
    here = ((ids >> 1) & 15) == z
    pick, turned = routing(jnp.where(here, (ids >> 5) * owned + (ids & 1), -1), LOCAL)
    present = jnp.sum(pick.astype(F32), axis=2).reshape(groups, LOCAL, -1)
    present = present.transpose(1, 0, 2).reshape(LOCAL, -1, 1)
    peers = jnp.arange(8, dtype=jnp.int32)
    order = peer_place(peers >> 2, peers & 3)

    pick, turned, present, order, dec_weight = tie(pick, turned, present, order, dec_weight)

    pieces, left = [], enc_bias
    for _ in range(3):
        piece = lax.reduce_precision(left, 8, 7)
        pieces.append(piece.astype(BF16))
        left = left - piece
    pieces = jnp.stack(pieces, 1)
    turned_enc = jnp.concatenate(
        [enc_weight.swapaxes(1, 2), jnp.pad(pieces, ((0, 0), (0, 13), (0, 0)))], axis=1
    )
    turned_enc = both(gather_half(turned_enc))
    dec_half = gather_half(dec_weight)
    bias_local = jnp.concatenate([w[:, width : width + 3] for w in turned_enc])
    bias_local = jnp.sum(bias_local.astype(F32)[:, ::-1], 1, keepdims=True)

    pick, bias_local = tie(pick, bias_local)
    pre_part, = project(order, pick, rows, *turned_enc, False)
    dec_half, pre_part = tie(dec_half, pre_part)
    dec_local = both(dec_half)
    pre, act, home = decode(order, pre_part, bias_local, turned, *dec_local)
    home, rows = tie(home, rows)
    total = lax.psum_scatter(
        home.reshape(NZ * tok_count, width), "z", scatter_dimension=0, tiled=True
    )

    owner_rows = to_owners(select(pick, rows))
    turned_dec = [w.swapaxes(1, 2) for w in dec_local]
    total, owner_rows, turned_dec = tie(total, owner_rows, turned_dec)
    recon = total.astype(F32) + dec_bias[None, :]
    reconstruction = recon.astype(BF16)
    error = (recon - residuals.astype(F32)).astype(BF16)
    errors = over_z(error)

    owner_act = to_owners(act)
    sig = jax.nn.sigmoid(pre) * present
    errors, owner_act, sig = tie(errors, owner_act, sig)

    dact, error_slots = project(order, pick, errors, *turned_dec, True)
    owner_errors = to_owners(error_slots)
    slope, owner_errors = tie(slopes(dact, sig), owner_errors)
    owner_slope = to_owners(slope)
    enc_grad, enc_bias_grad = outer(owner_slope, owner_rows)
    dec_grad, _ = outer(owner_act, owner_errors)
    return reconstruction, enc_grad, enc_bias_grad, dec_grad


def solution(mesh):
    fine = Mesh(mesh.devices.reshape(2, NY, NZ, 4), ("sect", "y", "z", "lat"))
    own = ("sect", "y", "z")
    return jax.shard_map(
        shards,
        mesh=fine,
        in_specs=(
            P(own, "lat"),
            P(own),
            P(own, None),
            P(own, None, "lat"),
            P(own, None),
            P(own, None, "lat"),
            P("lat"),
        ),
        out_specs=(
            P(own, "lat"),
            P(own, None, "lat"),
            P(own, None),
            P(own, None, "lat"),
        ),
        check_vma=False,
    )
```

```python
import jax
import jax.numpy as jnp
from jax import lax
from jax.experimental import pallas as pl
from jax.experimental.pallas import tpu as pltpu
from jax.sharding import Mesh, PartitionSpec as P

BLOCKS = 64
L1_COEF = 0.2
CAP = 4
NY = 4
NZ = 16
GROUP = 4
TILES = 3
LOCAL = 16

F32 = jnp.float32
BF16 = jnp.bfloat16


def swap_cores(v):
    return lax.ppermute(v, "sect", [(0, 1), (1, 0)])


def y_ring(v, step):
    perm = [(y, (y + step) % NY) for y in range(NY)]
    perm += [(NY + y, NY + (y - step) % NY) for y in range(NY)]
    return lax.ppermute(v, ("sect", "y"), perm)


def gather_half(own, early, late):
    chip = jnp.stack([own, swap_cores(own)])
    near, early = tie(y_ring(chip, 1), early)
    far, late = tie(y_ring(near[0], 1), late(early))
    return jnp.concatenate([own[None], near, far[None]]), late


def tie(*values):
    return lax.optimization_barrier(values)


def peer_place(owner_sect, owner_y):
    sect, y = lax.axis_index("sect"), lax.axis_index("y")
    other = owner_sect ^ sect
    delta = owner_y - y
    delta = jnp.where(sect == 0, delta, -delta) & 3
    code = delta * 2 + other
    place = jnp.zeros_like(code)
    for at, value in enumerate((0, 4, 6, 5, 3, 7, 1, 2)):
        place = jnp.where(code == at, value, place)
    return place


def routing(place, local):
    sources, _, toks = place.shape
    groups = sources // GROUP
    named = jnp.sum(
        (place[:, :, None, :] == jnp.arange(local, dtype=jnp.int32)[None, None, :, None]).astype(F32), 1
    )
    before = (jnp.arange(toks)[:, None] < jnp.arange(toks)[None, :]).astype(BF16)
    rank = jnp.einsum("skt,tu->sku", named.astype(BF16), before, preferred_element_type=F32)
    slot = rank + CAP * (jnp.arange(sources, dtype=jnp.int32) % GROUP).astype(F32)[:, None, None]
    slot = jnp.where(named > 0, slot, -1.0)
    slot = slot.reshape(groups, GROUP, local, toks).transpose(0, 2, 1, 3)
    slot = slot.reshape(groups, local, GROUP * toks)
    number = jnp.arange(GROUP * CAP, dtype=F32)
    pick = (slot[:, :, None, :] == number[None, None, :, None]).astype(BF16)
    turned = jnp.repeat(slot.transpose(0, 2, 1), GROUP * CAP, axis=2)
    turned = (turned == jnp.tile(number, local)[None, None, :]).astype(BF16)
    return pick.reshape(groups, -1, GROUP * toks), turned


def whole(*shape):
    return pl.BlockSpec(shape, lambda i: (0,) * len(shape))


def columns(*shape):
    return pl.BlockSpec(shape, lambda i: (0,) * (len(shape) - 1) + (i,))


PARAMS = pltpu.CompilerParams(
    dimension_semantics=("arbitrary",), vmem_limit_bytes=58 * 1024 * 1024
)


def take(pick, rows, slots):
    groups, wide, _ = pick.shape
    each = wide // LOCAL
    for q in range(groups):
        taken = jnp.dot(pick[q], rows[q], preferred_element_type=F32).astype(BF16)
        slots[:, q * each : (q + 1) * each, :] = taken.reshape(LOCAL, each, taken.shape[1])


def placed(order, wa, wb, k, owned):
    place = order[k // owned]
    at = (place & 3) * owned + k % owned
    return jnp.where(place < 4, wa[at], wb[at])


ORDER = pl.BlockSpec(memory_space=pltpu.SMEM)


def call(body, ins, in_specs, outs, out_specs, scratch, flops, moved):
    return pl.pallas_call(
        body,
        grid=(TILES,),
        in_specs=in_specs,
        out_specs=out_specs,
        out_shape=[jax.ShapeDtypeStruct(shape, kind) for shape, kind in outs],
        scratch_shapes=scratch,
        compiler_params=PARAMS,
        cost_estimate=pl.CostEstimate(flops=flops, bytes_accessed=moved, transcendentals=0),
    )(*ins)


def select(pick, rows):
    groups, wide, toks = pick.shape
    width = rows.shape[2]
    count = groups * wide // LOCAL
    return call(
        take,
        (pick, rows),
        [whole(groups, wide, toks), columns(groups, toks, width // TILES)],
        [((LOCAL, count, width), BF16)],
        [columns(LOCAL, count, width // TILES)],
        [],
        2 * groups * wide * toks * width,
        8_000_000,
    )[0]


def project_body(order, pick, rows, wa, wb, out, slots, total):
    step = pl.program_id(0)

    @pl.when(step == 0)
    def _():
        total[...] = jnp.zeros_like(total)

    take(pick, rows, slots)
    for k in range(LOCAL):
        w = placed(order, wa, wb, k, LOCAL // 8)
        total[k] = total[k] + jnp.dot(slots[k], w, preferred_element_type=F32)

    @pl.when(step == TILES - 1)
    def _():
        value = total[...].astype(BF16)
        for c in range(out.shape[0]):
            out[c] = value


def project(order, pick, rows, wa, wb, keep):
    groups, wide, toks = pick.shape
    half, _, latents = wa.shape
    width = rows.shape[2]
    tile = width // TILES
    count = groups * wide // LOCAL
    depth = pl.BlockSpec((half, tile, latents), lambda i: (0, i, 0))
    copies = 1 if keep else 4
    outs = [((copies, LOCAL, count, latents), BF16)]
    out_specs = [whole(copies, LOCAL, count, latents)]
    scratch = [pltpu.VMEM((LOCAL, count, latents), F32)]
    if keep:
        outs.append(((LOCAL, count, width), BF16))
        out_specs.append(columns(LOCAL, count, tile))
    else:
        scratch.insert(0, pltpu.VMEM((LOCAL, count, tile), BF16))
    return call(
        project_body,
        (order, pick, rows, wa, wb),
        [ORDER, whole(groups, wide, toks), columns(groups, toks, tile), depth, depth],
        outs,
        out_specs,
        scratch,
        2 * groups * wide * toks * width,
        12_000_000,
    )


def over_lat(part):
    return [part] + [
        lax.ppermute(part, "lat", [(i, (i + k) % 4) for i in range(4)]) for k in (1, 2, 3)
    ]


def sum_lat(a, b, c, d):
    return (a.astype(F32) + c.astype(F32)) + (b.astype(F32) + d.astype(F32))


def decode_body(order, copies, bias, turned, wa, wb, pre, act, home, part):
    groups, _, wide = turned.shape
    each = wide // LOCAL

    @pl.when(pl.program_id(0) == 0)
    def _():
        for k in range(LOCAL):
            owned = LOCAL // 8
            at = order[k // owned] * owned + k % owned
            value = sum_lat(*[copies[c, k] for c in range(4)]) + bias[at]
            pre[k] = value
            soft = jnp.maximum(value, 0.0) + jnp.log1p(jnp.exp(-jnp.abs(value)))
            act[k] = soft.astype(BF16)

    for k in range(LOCAL):
        w = placed(order, wa, wb, k, LOCAL // 8)
        part[k] = jnp.dot(act[k], w, preferred_element_type=F32).astype(BF16)
    for q in range(groups):
        rows = part[:, q * each : (q + 1) * each, :].reshape(wide, part.shape[2])
        home[q] = jnp.dot(turned[q], rows, preferred_element_type=F32).astype(BF16)


def decode(order, copies, bias, turned, wa, wb):
    groups, toks, wide = turned.shape
    half, latents, width = wa.shape
    tile = width // TILES
    count = groups * wide // LOCAL
    return call(
        decode_body,
        (order, copies, bias, turned, wa, wb),
        [
            ORDER,
            whole(4, LOCAL, count, latents),
            whole(LOCAL, 1, latents),
            whole(groups, toks, wide),
            columns(half, latents, tile),
            columns(half, latents, tile),
        ],
        [
            ((LOCAL, count, latents), F32),
            ((LOCAL, count, latents), BF16),
            ((groups, toks, width), BF16),
        ],
        [
            whole(LOCAL, count, latents),
            whole(LOCAL, count, latents),
            columns(groups, toks, tile),
        ],
        [pltpu.VMEM((LOCAL, count, tile), BF16)],
        2 * groups * wide * toks * width,
        12_000_000,
    )


def slope_body(a, b, c, d, sig, out):
    out[...] = ((sum_lat(a[...], b[...], c[...], d[...]) + L1_COEF) * sig[...]).astype(BF16)


def slopes(part, sig):
    return pl.pallas_call(
        slope_body,
        in_specs=[pl.BlockSpec(memory_space=pltpu.VMEM)] * 5,
        out_specs=pl.BlockSpec(memory_space=pltpu.VMEM),
        out_shape=jax.ShapeDtypeStruct(sig.shape, BF16),
        compiler_params=pltpu.CompilerParams(vmem_limit_bytes=16 * 1024 * 1024),
        cost_estimate=pl.CostEstimate(flops=0, bytes_accessed=2_500_000, transcendentals=0),
    )(*over_lat(part), sig)


def outer_body(values, rows, grad, sums, turned):
    peers, owned, count, tile = rows.shape

    @pl.when(pl.program_id(0) == 0)
    def _():
        for i in range(owned):
            value = values[:, i].reshape(peers * count, values.shape[3]).astype(F32)
            sums[i, :] = jnp.sum(value, 0)
            turned[i] = value.T.astype(BF16)

    for i in range(owned):
        grad[i] = jnp.dot(
            turned[i], rows[:, i].reshape(peers * count, tile), preferred_element_type=F32
        ).astype(BF16)


def outer(values, rows):
    peers, owned, count, width = rows.shape
    latents = values.shape[3]
    tile = width // TILES
    return call(
        outer_body,
        (values, rows),
        [whole(peers, owned, count, latents), columns(peers, owned, count, tile)],
        [((owned, latents, width), BF16), ((owned, latents), F32)],
        [columns(owned, latents, tile), whole(owned, latents)],
        [pltpu.VMEM((owned, latents, peers * count), BF16)],
        4 * peers * count * width * latents,
        5_000_000,
    )


def shards(residuals, routes, blocks, enc_weight, enc_bias, dec_weight, dec_bias):
    tok_count, width = residuals.shape
    owned, latents, _ = enc_weight.shape
    half = LOCAL // 2
    groups = NZ // GROUP
    z = lax.axis_index("z")

    def both(part):
        return [h.reshape(half, *h.shape[2:]) for h in (part, swap_cores(part))]

    def to_owners(v):
        return lax.all_to_all(
            v.reshape(8, owned, *v.shape[1:]), ("sect", "y"), 0, 0, tiled=True
        )

    def over_z(v):
        v = lax.all_gather(v, "z", axis=0, tiled=True)
        return v.reshape(groups, GROUP * tok_count, width)

    rows = over_z(residuals)

    global_block = (routes[:, None] * BLOCKS + blocks).T.reshape(1, 4, tok_count)
    ids = lax.all_to_all(
        jnp.broadcast_to(global_block, (NZ, 4, tok_count)), "z", 0, 0, tiled=True
    )

    def tables(ids):
        here = ((ids >> 1) & 15) == z
        pick, turned = routing(jnp.where(here, (ids >> 5) * owned + (ids & 1), -1), LOCAL)
        present = jnp.sum(pick.astype(F32), axis=2).reshape(groups, LOCAL, -1)
        present = present.transpose(1, 0, 2).reshape(LOCAL, -1, 1)
        peers = jnp.arange(8, dtype=jnp.int32)
        return pick, turned, present, peer_place(peers >> 2, peers & 3)

    pieces, left = [], enc_bias
    for _ in range(3):
        piece = lax.reduce_precision(left, 8, 7)
        pieces.append(piece.astype(BF16))
        left = left - piece
    pieces = jnp.stack(pieces, 1)
    turned_enc = jnp.concatenate(
        [enc_weight.swapaxes(1, 2), jnp.pad(pieces, ((0, 0), (0, 13), (0, 0)))], axis=1
    )
    turned_enc = both(gather_half(turned_enc, (), lambda v: v)[0])
    dec_half, (pick, turned, present, order) = gather_half(dec_weight, ids, tables)
    bias_local = jnp.concatenate([w[:, width : width + 3] for w in turned_enc])
    bias_local = jnp.sum(bias_local.astype(F32)[:, ::-1], 1, keepdims=True)

    pick, bias_local = tie(pick, bias_local)
    pre_part, = project(order, pick, rows, *turned_enc, False)
    dec_local = both(dec_half)
    copies = lax.all_to_all(pre_part, "lat", 0, 0, tiled=True)
    pre, act, home = decode(order, copies, bias_local, turned, *dec_local)
    home, rows = tie(home, rows)
    total = lax.psum_scatter(
        home.reshape(NZ * tok_count, width), "z", scatter_dimension=0, tiled=True
    )

    owner_rows = to_owners(select(pick, rows))
    turned_dec = [w.swapaxes(1, 2) for w in dec_local]
    total, owner_rows, turned_dec = tie(total, owner_rows, turned_dec)
    recon = total.astype(F32) + dec_bias[None, :]
    reconstruction = recon.astype(BF16)
    error = (recon - residuals.astype(F32)).astype(BF16)
    errors = over_z(error)

    owner_act = to_owners(act)
    sig = jax.nn.sigmoid(pre) * present
    errors, owner_act, sig = tie(errors, owner_act, sig)

    dact, error_slots = project(order, pick, errors, *turned_dec, True)
    owner_errors = to_owners(error_slots)
    slope, owner_errors = tie(slopes(dact[0], sig), owner_errors)
    owner_slope = to_owners(slope)
    enc_grad, enc_bias_grad = outer(owner_slope, owner_rows)
    dec_grad, _ = outer(owner_act, owner_errors)
    return reconstruction, enc_grad, enc_bias_grad, dec_grad


def solution(mesh):
    fine = Mesh(mesh.devices.reshape(2, NY, NZ, 4), ("sect", "y", "z", "lat"))
    own = ("sect", "y", "z")
    return jax.shard_map(
        shards,
        mesh=fine,
        in_specs=(
            P(own, "lat"),
            P(own),
            P(own, None),
            P(own, None, "lat"),
            P(own, None),
            P(own, None, "lat"),
            P("lat"),
        ),
        out_specs=(
            P(own, "lat"),
            P(own, None, "lat"),
            P(own, None),
            P(own, None, "lat"),
        ),
        check_vma=False,
    )
```

```python
import jax
import jax.numpy as jnp
from jax import lax
from jax.experimental import pallas as pl
from jax.experimental.pallas import tpu as pltpu
from jax.sharding import Mesh, PartitionSpec as P

BLOCKS = 64
L1_COEF = 0.2
CAP = 4
NY = 4
NZ = 16
GROUP = 4
TILES = 3
LOCAL = 16

F32 = jnp.float32
BF16 = jnp.bfloat16


def swap_cores(v):
    return lax.ppermute(v, "sect", [(0, 1), (1, 0)])


def y_ring(v, step):
    perm = [(y, (y + step) % NY) for y in range(NY)]
    perm += [(NY + y, NY + (y - step) % NY) for y in range(NY)]
    return lax.ppermute(v, ("sect", "y"), perm)


def gather_half(own, early, late):
    chip = jnp.stack([own, swap_cores(own)])
    near, early = tie(y_ring(chip, 1), early)
    far, late = tie(y_ring(near[0], 1), late(early))
    return jnp.concatenate([own[None], near, far[None]]), late


def tie(*values):
    return lax.optimization_barrier(values)


def peer_place(owner_sect, owner_y):
    sect, y = lax.axis_index("sect"), lax.axis_index("y")
    other = owner_sect ^ sect
    delta = owner_y - y
    delta = jnp.where(sect == 0, delta, -delta) & 3
    code = delta * 2 + other
    place = jnp.zeros_like(code)
    for at, value in enumerate((0, 4, 6, 5, 3, 7, 1, 2)):
        place = jnp.where(code == at, value, place)
    return place


def routing(place, local):
    sources, _, toks = place.shape
    groups = sources // GROUP
    named = jnp.sum(
        (place[:, :, None, :] == jnp.arange(local, dtype=jnp.int32)[None, None, :, None]).astype(F32), 1
    )
    before = (jnp.arange(toks)[:, None] < jnp.arange(toks)[None, :]).astype(BF16)
    rank = jnp.einsum("skt,tu->sku", named.astype(BF16), before, preferred_element_type=F32)
    slot = rank + CAP * (jnp.arange(sources, dtype=jnp.int32) % GROUP).astype(F32)[:, None, None]
    slot = jnp.where(named > 0, slot, -1.0)
    slot = slot.reshape(groups, GROUP, local, toks).transpose(0, 2, 1, 3)
    slot = slot.reshape(groups, local, GROUP * toks)
    number = jnp.arange(GROUP * CAP, dtype=F32)
    pick = (slot[:, :, None, :] == number[None, None, :, None]).astype(BF16)
    turned = jnp.repeat(slot.transpose(0, 2, 1), GROUP * CAP, axis=2)
    turned = (turned == jnp.tile(number, local)[None, None, :]).astype(BF16)
    return pick.reshape(groups, -1, GROUP * toks), turned


def whole(*shape):
    return pl.BlockSpec(shape, lambda i: (0,) * len(shape))


def columns(*shape):
    return pl.BlockSpec(shape, lambda i: (0,) * (len(shape) - 1) + (i,))


PARAMS = pltpu.CompilerParams(
    dimension_semantics=("arbitrary",), vmem_limit_bytes=58 * 1024 * 1024
)


def take(pick, rows, slots):
    groups, wide, _ = pick.shape
    each = wide // LOCAL
    for q in range(groups):
        taken = jnp.dot(pick[q], rows[q], preferred_element_type=F32).astype(BF16)
        slots[:, q * each : (q + 1) * each, :] = taken.reshape(LOCAL, each, taken.shape[1])


def placed(order, wa, wb, k, owned):
    place = order[k // owned]
    at = (place & 3) * owned + k % owned
    return jnp.where(place < 4, wa[at], wb[at])


ORDER = pl.BlockSpec(memory_space=pltpu.SMEM)


def call(steps, body, ins, in_specs, outs, out_specs, scratch, flops, moved):
    return pl.pallas_call(
        body,
        grid=(steps,),
        in_specs=in_specs,
        out_specs=out_specs,
        out_shape=[jax.ShapeDtypeStruct(shape, kind) for shape, kind in outs],
        scratch_shapes=scratch,
        compiler_params=PARAMS,
        cost_estimate=pl.CostEstimate(flops=flops, bytes_accessed=moved, transcendentals=0),
    )(*ins)


def select(pick, rows):
    groups, wide, toks = pick.shape
    width = rows.shape[2]
    count = groups * wide // LOCAL
    return call(
        TILES,
        take,
        (pick, rows),
        [whole(groups, wide, toks), columns(groups, toks, width // TILES)],
        [((LOCAL, count, width), BF16)],
        [columns(LOCAL, count, width // TILES)],
        [],
        2 * groups * wide * toks * width,
        8_000_000,
    )[0]


def start(*pairs):
    copies = [pltpu.make_async_copy(*pair) for pair in pairs]
    for copy in copies:
        copy.start()
    return copies


ANY = pl.BlockSpec(memory_space=pl.ANY)
VMEM = pl.BlockSpec(memory_space=pltpu.VMEM)


def staged(body, ins, in_specs, outs, out_specs, scratch, flops, moved):
    return pl.pallas_call(
        body,
        in_specs=in_specs,
        out_specs=out_specs,
        out_shape=[jax.ShapeDtypeStruct(shape, kind) for shape, kind in outs],
        scratch_shapes=scratch,
        compiler_params=pltpu.CompilerParams(vmem_limit_bytes=58 * 1024 * 1024),
        cost_estimate=pl.CostEstimate(flops=flops, bytes_accessed=moved, transcendentals=0),
    )(*ins)


def project_body(keep, order, pick, rows, wa, wb, out, *refs):
    if keep:
        kept, *refs = refs
    held, moved, va, vb, slots, sems = refs
    groups, wide, _ = pick.shape
    each = wide // LOCAL
    width = rows.shape[2]
    parts = [
        start((pick.at[q], held.at[q], sems.at[0, q]), (rows.at[q], moved.at[q], sems.at[1, q]))
        for q in range(groups)
    ]
    weights = start(
        (wa.at[:, pl.ds(0, width)], va, sems.at[2, 0]),
        (wb.at[:, pl.ds(0, width)], vb, sems.at[2, 1]),
    )
    for q in range(groups):
        for copy in parts[q]:
            copy.wait()
        taken = jnp.dot(held[q], moved[q], preferred_element_type=F32).astype(BF16)
        slots[:, q * each : (q + 1) * each, :] = taken.reshape(LOCAL, each, width)
    leaving = start((slots, kept, sems.at[2, 2])) if keep else []
    for copy in weights:
        copy.wait()
    for k in range(LOCAL):
        w = placed(order, va, vb, k, LOCAL // 8)
        value = jnp.dot(slots[k], w, preferred_element_type=F32).astype(BF16)
        for c in range(out.shape[0]):
            out[c, k] = value
    for copy in leaving:
        copy.wait()


def project(order, pick, rows, wa, wb, keep):
    groups, wide, toks = pick.shape
    half, _, latents = wa.shape
    width = rows.shape[2]
    count = groups * wide // LOCAL
    outs = [((1 if keep else 4, LOCAL, count, latents), BF16)]
    if keep:
        outs.append(((LOCAL, count, width), BF16))
    return staged(
        lambda *refs: project_body(keep, *refs),
        (order, pick, rows, wa, wb),
        [ORDER] + [ANY] * 4,
        outs,
        [VMEM, ANY][: len(outs)],
        [
            pltpu.VMEM((groups, wide, toks), BF16),
            pltpu.VMEM((groups, toks, width), BF16),
            pltpu.VMEM((half, width, latents), BF16),
            pltpu.VMEM((half, width, latents), BF16),
            pltpu.VMEM((LOCAL, count, width), BF16),
            pltpu.SemaphoreType.DMA((3, 4)),
        ],
        2 * groups * wide * toks * width,
        12_000_000,
    )


def decode_body(order, copies, bias, turned, wa, wb, pre, act, home, got, held, va, vb, part, done, sems):
    groups, _, wide = turned.shape
    each = wide // LOCAL
    first = start((copies, got, sems.at[0, 0]))
    weights = start((wa, va, sems.at[0, 1]), (wb, vb, sems.at[0, 2]))
    tables = start((turned, held, sems.at[0, 3]))
    for copy in first:
        copy.wait()
    owned = LOCAL // 8
    for k in range(LOCAL):
        at = order[k // owned] * owned + k % owned
        value = sum_lat(*[got[c, k] for c in range(4)]) + bias[at]
        pre[k] = value
        soft = jnp.maximum(value, 0.0) + jnp.log1p(jnp.exp(-jnp.abs(value)))
        act[k] = soft.astype(BF16)
    for copy in weights:
        copy.wait()
    for k in range(LOCAL):
        w = placed(order, va, vb, k, owned)
        part[k] = jnp.dot(act[k], w, preferred_element_type=F32).astype(BF16)
    for copy in tables:
        copy.wait()
    leaving = []
    for q in range(groups):
        rows = part[:, q * each : (q + 1) * each, :].reshape(wide, part.shape[2])
        done[q] = jnp.dot(held[q], rows, preferred_element_type=F32).astype(BF16)
        leaving += start((done.at[q], home.at[q], sems.at[1, q]))
    for copy in leaving:
        copy.wait()


def decode(order, copies, bias, turned, wa, wb):
    groups, toks, wide = turned.shape
    half, latents, width = wa.shape
    count = groups * wide // LOCAL
    return staged(
        decode_body,
        (order, copies, bias, turned, wa, wb),
        [ORDER, ANY, VMEM, ANY, ANY, ANY],
        [
            ((LOCAL, count, latents), F32),
            ((LOCAL, count, latents), BF16),
            ((groups, toks, width), BF16),
        ],
        [VMEM, VMEM, ANY],
        [
            pltpu.VMEM((4, LOCAL, count, latents), BF16),
            pltpu.VMEM((groups, toks, wide), BF16),
            pltpu.VMEM((half, latents, width), BF16),
            pltpu.VMEM((half, latents, width), BF16),
            pltpu.VMEM((LOCAL, count, width), BF16),
            pltpu.VMEM((groups, toks, width), BF16),
            pltpu.SemaphoreType.DMA((2, 4)),
        ],
        2 * groups * wide * toks * width,
        12_000_000,
    )


def over_lat(part):
    return [part] + [
        lax.ppermute(part, "lat", [(i, (i + k) % 4) for i in range(4)]) for k in (1, 2, 3)
    ]


def sum_lat(a, b, c, d):
    return (a.astype(F32) + c.astype(F32)) + (b.astype(F32) + d.astype(F32))


def slope_body(a, b, c, d, sig, out):
    out[...] = ((sum_lat(a[...], b[...], c[...], d[...]) + L1_COEF) * sig[...]).astype(BF16)


def slopes(part, sig):
    return pl.pallas_call(
        slope_body,
        in_specs=[pl.BlockSpec(memory_space=pltpu.VMEM)] * 5,
        out_specs=pl.BlockSpec(memory_space=pltpu.VMEM),
        out_shape=jax.ShapeDtypeStruct(sig.shape, BF16),
        compiler_params=pltpu.CompilerParams(vmem_limit_bytes=16 * 1024 * 1024),
        cost_estimate=pl.CostEstimate(flops=0, bytes_accessed=2_500_000, transcendentals=0),
    )(*over_lat(part), sig)


def outer_body(values, rows, grad, sums, turned):
    peers, owned, count, tile = rows.shape

    @pl.when(pl.program_id(0) == 0)
    def _():
        for i in range(owned):
            value = values[:, i].reshape(peers * count, values.shape[3]).astype(F32)
            sums[i, :] = jnp.sum(value, 0)
            turned[i] = value.T.astype(BF16)

    for i in range(owned):
        grad[i] = jnp.dot(
            turned[i], rows[:, i].reshape(peers * count, tile), preferred_element_type=F32
        ).astype(BF16)


def outer(values, rows):
    peers, owned, count, width = rows.shape
    latents = values.shape[3]
    return call(
        1,
        outer_body,
        (values, rows),
        [whole(peers, owned, count, latents), columns(peers, owned, count, width)],
        [((owned, latents, width), BF16), ((owned, latents), F32)],
        [columns(owned, latents, width), whole(owned, latents)],
        [pltpu.VMEM((owned, latents, peers * count), BF16)],
        4 * peers * count * width * latents,
        5_000_000,
    )


def shards(residuals, routes, blocks, enc_weight, enc_bias, dec_weight, dec_bias):
    tok_count, width = residuals.shape
    owned, latents, _ = enc_weight.shape
    half = LOCAL // 2
    groups = NZ // GROUP
    z = lax.axis_index("z")

    def both(part):
        return [h.reshape(half, *h.shape[2:]) for h in (part, swap_cores(part))]

    def to_owners(v):
        return lax.all_to_all(
            v.reshape(8, owned, *v.shape[1:]), ("sect", "y"), 0, 0, tiled=True
        )

    def over_z(v):
        v = lax.all_gather(v, "z", axis=0, tiled=True)
        return v.reshape(groups, GROUP * tok_count, width)

    rows = over_z(residuals)

    global_block = (routes[:, None] * BLOCKS + blocks).T.reshape(1, 4, tok_count)
    ids = lax.all_to_all(
        jnp.broadcast_to(global_block, (NZ, 4, tok_count)), "z", 0, 0, tiled=True
    )

    def tables(ids):
        here = ((ids >> 1) & 15) == z
        pick, turned = routing(jnp.where(here, (ids >> 5) * owned + (ids & 1), -1), LOCAL)
        present = jnp.sum(pick.astype(F32), axis=2).reshape(groups, LOCAL, -1)
        present = present.transpose(1, 0, 2).reshape(LOCAL, -1, 1)
        peers = jnp.arange(8, dtype=jnp.int32)
        return pick, turned, present, peer_place(peers >> 2, peers & 3)

    pieces, left = [], enc_bias
    for _ in range(3):
        piece = lax.reduce_precision(left, 8, 7)
        pieces.append(piece.astype(BF16))
        left = left - piece
    pieces = jnp.stack(pieces, 1)
    turned_enc = jnp.concatenate(
        [enc_weight.swapaxes(1, 2), jnp.pad(pieces, ((0, 0), (0, 13), (0, 0)))], axis=1
    )
    turned_enc = both(gather_half(turned_enc, (), lambda v: v)[0])
    dec_half, (pick, turned, present, order) = gather_half(dec_weight, ids, tables)
    bias_local = jnp.concatenate([w[:, width : width + 3] for w in turned_enc])
    bias_local = jnp.sum(bias_local.astype(F32)[:, ::-1], 1, keepdims=True)

    pick, bias_local = tie(pick, bias_local)
    pre_part, = project(order, pick, rows, *turned_enc, False)
    dec_local = both(dec_half)
    copies = lax.all_to_all(pre_part, "lat", 0, 0, tiled=True)
    pre, act, home = decode(order, copies, bias_local, turned, *dec_local)
    home, rows = tie(home, rows)
    total = lax.psum_scatter(
        home.reshape(NZ * tok_count, width), "z", scatter_dimension=0, tiled=True
    )

    owner_rows = to_owners(select(pick, rows))
    turned_dec = [w.swapaxes(1, 2) for w in dec_local]
    total, owner_rows, turned_dec = tie(total, owner_rows, turned_dec)
    recon = total.astype(F32) + dec_bias[None, :]
    reconstruction = recon.astype(BF16)
    error = (recon - residuals.astype(F32)).astype(BF16)
    errors = over_z(error)

    owner_act = to_owners(act)
    sig = jax.nn.sigmoid(pre) * present
    errors, owner_act, sig = tie(errors, owner_act, sig)

    dact, error_slots = project(order, pick, errors, *turned_dec, True)
    owner_errors = to_owners(error_slots)
    slope, owner_errors = tie(slopes(dact[0], sig), owner_errors)
    owner_slope = to_owners(slope)
    enc_grad, enc_bias_grad = outer(owner_slope, owner_rows)
    dec_grad, _ = outer(owner_act, owner_errors)
    return reconstruction, enc_grad, enc_bias_grad, dec_grad


def solution(mesh):
    fine = Mesh(mesh.devices.reshape(2, NY, NZ, 4), ("sect", "y", "z", "lat"))
    own = ("sect", "y", "z")
    return jax.shard_map(
        shards,
        mesh=fine,
        in_specs=(
            P(own, "lat"),
            P(own),
            P(own, None),
            P(own, None, "lat"),
            P(own, None),
            P(own, None, "lat"),
            P("lat"),
        ),
        out_specs=(
            P(own, "lat"),
            P(own, None, "lat"),
            P(own, None),
            P(own, None, "lat"),
        ),
        check_vma=False,
    )
```

```python
import jax
import jax.numpy as jnp
from jax import lax
from jax.experimental import pallas as pl
from jax.experimental.pallas import tpu as pltpu
from jax.sharding import Mesh, PartitionSpec as P

BLOCKS = 64
L1_COEF = 0.2
CAP = 4
NY = 4
NZ = 16
GROUP = 4
TILES = 3
LOCAL = 16

F32 = jnp.float32
BF16 = jnp.bfloat16


def swap_cores(v):
    return lax.ppermute(v, "sect", [(0, 1), (1, 0)])


def y_ring(v, step):
    perm = [(y, (y + step) % NY) for y in range(NY)]
    perm += [(NY + y, NY + (y - step) % NY) for y in range(NY)]
    return lax.ppermute(v, ("sect", "y"), perm)


def gather_half(own, early, late):
    chip = jnp.stack([own, swap_cores(own)])
    near, early = tie(y_ring(chip, 1), early)
    far, late = tie(y_ring(near[0], 1), late(early))
    return jnp.concatenate([own[None], near, far[None]]), late


def tie(*values):
    return lax.optimization_barrier(values)


def peer_place(owner_sect, owner_y):
    sect, y = lax.axis_index("sect"), lax.axis_index("y")
    other = owner_sect ^ sect
    delta = owner_y - y
    delta = jnp.where(sect == 0, delta, -delta) & 3
    code = delta * 2 + other
    place = jnp.zeros_like(code)
    for at, value in enumerate((0, 4, 6, 5, 3, 7, 1, 2)):
        place = jnp.where(code == at, value, place)
    return place


def routing(place, local):
    sources, _, toks = place.shape
    groups = sources // GROUP
    named = jnp.sum(
        (place[:, :, None, :] == jnp.arange(local, dtype=jnp.int32)[None, None, :, None]).astype(F32), 1
    )
    before = (jnp.arange(toks)[:, None] < jnp.arange(toks)[None, :]).astype(BF16)
    rank = jnp.einsum("skt,tu->sku", named.astype(BF16), before, preferred_element_type=F32)
    slot = rank + CAP * (jnp.arange(sources, dtype=jnp.int32) % GROUP).astype(F32)[:, None, None]
    slot = jnp.where(named > 0, slot, -1.0)
    slot = slot.reshape(groups, GROUP, local, toks).transpose(0, 2, 1, 3)
    slot = slot.reshape(groups, local, GROUP * toks)
    number = jnp.arange(GROUP * CAP, dtype=F32)
    pick = (slot[:, :, None, :] == number[None, None, :, None]).astype(BF16)
    turned = jnp.repeat(slot.transpose(0, 2, 1), GROUP * CAP, axis=2)
    turned = (turned == jnp.tile(number, local)[None, None, :]).astype(BF16)
    return pick.reshape(groups, -1, GROUP * toks), turned


def whole(*shape):
    return pl.BlockSpec(shape, lambda i: (0,) * len(shape))


def columns(*shape):
    return pl.BlockSpec(shape, lambda i: (0,) * (len(shape) - 1) + (i,))


PARAMS = pltpu.CompilerParams(
    dimension_semantics=("arbitrary",), vmem_limit_bytes=58 * 1024 * 1024
)


def take(pick, rows, slots):
    groups, wide, _ = pick.shape
    each = wide // LOCAL
    for q in range(groups):
        taken = jnp.dot(pick[q], rows[q], preferred_element_type=F32).astype(BF16)
        slots[:, q * each : (q + 1) * each, :] = taken.reshape(LOCAL, each, taken.shape[1])


def placed(order, wa, wb, k, owned):
    place = order[k // owned]
    at = (place & 3) * owned + k % owned
    return jnp.where(place < 4, wa[at], wb[at])


ORDER = pl.BlockSpec(memory_space=pltpu.SMEM)


def call(steps, body, ins, in_specs, outs, out_specs, scratch, flops, moved):
    return pl.pallas_call(
        body,
        grid=(steps,),
        in_specs=in_specs,
        out_specs=out_specs,
        out_shape=[jax.ShapeDtypeStruct(shape, kind) for shape, kind in outs],
        scratch_shapes=scratch,
        compiler_params=PARAMS,
        cost_estimate=pl.CostEstimate(flops=flops, bytes_accessed=moved, transcendentals=0),
    )(*ins)


def select(pick, rows):
    groups, wide, toks = pick.shape
    width = rows.shape[2]
    count = groups * wide // LOCAL
    return call(
        TILES,
        take,
        (pick, rows),
        [whole(groups, wide, toks), columns(groups, toks, width // TILES)],
        [((LOCAL, count, width), BF16)],
        [columns(LOCAL, count, width // TILES)],
        [],
        2 * groups * wide * toks * width,
        8_000_000,
    )[0]


def start(*pairs):
    copies = [pltpu.make_async_copy(*pair) for pair in pairs]
    for copy in copies:
        copy.start()
    return copies


ANY = pl.BlockSpec(memory_space=pl.ANY)
VMEM = pl.BlockSpec(memory_space=pltpu.VMEM)


def staged(body, ins, in_specs, outs, out_specs, scratch, flops, moved):
    return pl.pallas_call(
        body,
        in_specs=in_specs,
        out_specs=out_specs,
        out_shape=[jax.ShapeDtypeStruct(shape, kind) for shape, kind in outs],
        scratch_shapes=scratch,
        compiler_params=pltpu.CompilerParams(vmem_limit_bytes=58 * 1024 * 1024),
        cost_estimate=pl.CostEstimate(flops=flops, bytes_accessed=moved, transcendentals=0),
    )(*ins)


def project_body(keep, order, pick, rows, wa, wb, out, *refs):
    if keep:
        kept, *refs = refs
    held, moved, va, vb, slots, sems = refs
    groups, wide, _ = pick.shape
    each = wide // LOCAL
    width = rows.shape[2]
    parts = [
        start((pick.at[q], held.at[q], sems.at[0, q]), (rows.at[q], moved.at[q], sems.at[1, q]))
        for q in range(groups)
    ]
    weights = start(
        (wa.at[:, pl.ds(0, width)], va, sems.at[2, 0]),
        (wb.at[:, pl.ds(0, width)], vb, sems.at[2, 1]),
    )
    for q in range(groups):
        for copy in parts[q]:
            copy.wait()
        taken = jnp.dot(held[q], moved[q], preferred_element_type=F32).astype(BF16)
        slots[:, q * each : (q + 1) * each, :] = taken.reshape(LOCAL, each, width)
    leaving = start((slots, kept, sems.at[2, 2])) if keep else []
    for copy in weights:
        copy.wait()
    for k in range(LOCAL):
        w = placed(order, va, vb, k, LOCAL // 8)
        value = jnp.dot(slots[k], w, preferred_element_type=F32).astype(BF16)
        for c in range(out.shape[0]):
            out[c, k] = value
    for copy in leaving:
        copy.wait()


def project(order, pick, rows, wa, wb, keep):
    groups, wide, toks = pick.shape
    half, _, latents = wa.shape
    width = rows.shape[2]
    count = groups * wide // LOCAL
    outs = [((1 if keep else 4, LOCAL, count, latents), BF16)]
    if keep:
        outs.append(((LOCAL, count, width), BF16))
    return staged(
        lambda *refs: project_body(keep, *refs),
        (order, pick, rows, wa, wb),
        [ORDER] + [ANY] * 4,
        outs,
        [VMEM, ANY][: len(outs)],
        [
            pltpu.VMEM((groups, wide, toks), BF16),
            pltpu.VMEM((groups, toks, width), BF16),
            pltpu.VMEM((half, width, latents), BF16),
            pltpu.VMEM((half, width, latents), BF16),
            pltpu.VMEM((LOCAL, count, width), BF16),
            pltpu.SemaphoreType.DMA((3, 4)),
        ],
        2 * groups * wide * toks * width,
        12_000_000,
    )


def decode_body(order, copies, bias, turned, wa, wb, pre, act, home, got, held, va, vb, part, done, sems):
    groups, _, wide = turned.shape
    each = wide // LOCAL
    first = start((copies, got, sems.at[0, 0]))
    weights = start((wa, va, sems.at[0, 1]), (wb, vb, sems.at[0, 2]))
    tables = start((turned, held, sems.at[0, 3]))
    for copy in first:
        copy.wait()
    owned = LOCAL // 8
    for k in range(LOCAL):
        at = order[k // owned] * owned + k % owned
        value = sum_lat(*[got[c, k] for c in range(4)]) + bias[at]
        pre[k] = value
        soft = jnp.maximum(value, 0.0) + jnp.log1p(jnp.exp(-jnp.abs(value)))
        act[k] = soft.astype(BF16)
    for copy in weights:
        copy.wait()
    for k in range(LOCAL):
        w = placed(order, va, vb, k, owned)
        part[k] = jnp.dot(act[k], w, preferred_element_type=F32).astype(BF16)
    for copy in tables:
        copy.wait()
    leaving = []
    for q in range(groups):
        rows = part[:, q * each : (q + 1) * each, :].reshape(wide, part.shape[2])
        done[q] = jnp.dot(held[q], rows, preferred_element_type=F32).astype(BF16)
        leaving += start((done.at[q], home.at[q], sems.at[1, q]))
    for copy in leaving:
        copy.wait()


def decode(order, copies, bias, turned, wa, wb):
    groups, toks, wide = turned.shape
    half, latents, width = wa.shape
    count = groups * wide // LOCAL
    return staged(
        decode_body,
        (order, copies, bias, turned, wa, wb),
        [ORDER, ANY, VMEM, ANY, ANY, ANY],
        [
            ((LOCAL, count, latents), F32),
            ((LOCAL, count, latents), BF16),
            ((groups, toks, width), BF16),
        ],
        [VMEM, VMEM, ANY],
        [
            pltpu.VMEM((4, LOCAL, count, latents), BF16),
            pltpu.VMEM((groups, toks, wide), BF16),
            pltpu.VMEM((half, latents, width), BF16),
            pltpu.VMEM((half, latents, width), BF16),
            pltpu.VMEM((LOCAL, count, width), BF16),
            pltpu.VMEM((groups, toks, width), BF16),
            pltpu.SemaphoreType.DMA((2, 4)),
        ],
        2 * groups * wide * toks * width,
        12_000_000,
    )


def pick_body(pick, rows, out, held, moved, sems):
    groups, wide, _ = pick.shape
    each = wide // LOCAL
    parts = [
        start((pick.at[q], held.at[q], sems.at[0, q]), (rows.at[q], moved.at[q], sems.at[1, q]))
        for q in range(groups)
    ]
    for q in range(groups):
        for copy in parts[q]:
            copy.wait()
        taken = jnp.dot(held[q], moved[q], preferred_element_type=F32).astype(BF16)
        out[:, q * each : (q + 1) * each, :] = taken.reshape(LOCAL, each, rows.shape[2])


def pick_slots(pick, rows):
    groups, wide, toks = pick.shape
    width = rows.shape[2]
    return staged(
        pick_body,
        (pick, rows),
        [ANY, ANY],
        [((LOCAL, groups * wide // LOCAL, width), BF16)],
        [VMEM],
        [
            pltpu.VMEM((groups, wide, toks), BF16),
            pltpu.VMEM((groups, toks, width), BF16),
            pltpu.SemaphoreType.DMA((2, 4)),
        ],
        2 * groups * wide * toks * width,
        8_000_000,
    )[0]


def inward_body(order, slots, wa, wb, out, held, va, vb, sems):
    copies = start((slots, held, sems.at[0]), (wa, va, sems.at[1]), (wb, vb, sems.at[2]))
    for copy in copies:
        copy.wait()
    for k in range(LOCAL):
        w = placed(order, va, vb, k, LOCAL // 8)
        out[k] = jnp.dot(held[k], w, preferred_element_type=F32).astype(BF16)


def inward(order, slots, wa, wb):
    _, count, width = slots.shape
    half, _, latents = wa.shape
    return staged(
        inward_body,
        (order, slots, wa, wb),
        [ORDER, ANY, ANY, ANY],
        [((LOCAL, count, latents), BF16)],
        [VMEM],
        [
            pltpu.VMEM((LOCAL, count, width), BF16),
            pltpu.VMEM((half, width, latents), BF16),
            pltpu.VMEM((half, width, latents), BF16),
            pltpu.SemaphoreType.DMA((3,)),
        ],
        2 * LOCAL * count * width * latents,
        8_000_000,
    )[0]


def over_lat(part):
    return [part] + [
        lax.ppermute(part, "lat", [(i, (i + k) % 4) for i in range(4)]) for k in (1, 2, 3)
    ]


def sum_lat(a, b, c, d):
    return (a.astype(F32) + c.astype(F32)) + (b.astype(F32) + d.astype(F32))


def slope_body(a, b, c, d, sig, out):
    out[...] = ((sum_lat(a[...], b[...], c[...], d[...]) + L1_COEF) * sig[...]).astype(BF16)


def slopes(part, sig):
    return pl.pallas_call(
        slope_body,
        in_specs=[pl.BlockSpec(memory_space=pltpu.VMEM)] * 5,
        out_specs=pl.BlockSpec(memory_space=pltpu.VMEM),
        out_shape=jax.ShapeDtypeStruct(sig.shape, BF16),
        compiler_params=pltpu.CompilerParams(vmem_limit_bytes=16 * 1024 * 1024),
        cost_estimate=pl.CostEstimate(flops=0, bytes_accessed=2_500_000, transcendentals=0),
    )(*over_lat(part), sig)


def outer_body(values, rows, grad, sums, turned):
    peers, owned, count, tile = rows.shape

    @pl.when(pl.program_id(0) == 0)
    def _():
        for i in range(owned):
            value = values[:, i].reshape(peers * count, values.shape[3]).astype(F32)
            sums[i, :] = jnp.sum(value, 0)
            turned[i] = value.T.astype(BF16)

    for i in range(owned):
        grad[i] = jnp.dot(
            turned[i], rows[:, i].reshape(peers * count, tile), preferred_element_type=F32
        ).astype(BF16)


def outer(values, rows):
    peers, owned, count, width = rows.shape
    latents = values.shape[3]
    return call(
        1,
        outer_body,
        (values, rows),
        [whole(peers, owned, count, latents), columns(peers, owned, count, width)],
        [((owned, latents, width), BF16), ((owned, latents), F32)],
        [columns(owned, latents, width), whole(owned, latents)],
        [pltpu.VMEM((owned, latents, peers * count), BF16)],
        4 * peers * count * width * latents,
        5_000_000,
    )


def shards(residuals, routes, blocks, enc_weight, enc_bias, dec_weight, dec_bias):
    tok_count, width = residuals.shape
    owned, latents, _ = enc_weight.shape
    half = LOCAL // 2
    groups = NZ // GROUP
    z = lax.axis_index("z")

    def both(part):
        return [h.reshape(half, *h.shape[2:]) for h in (part, swap_cores(part))]

    def to_owners(v):
        return lax.all_to_all(
            v.reshape(8, owned, *v.shape[1:]), ("sect", "y"), 0, 0, tiled=True
        )

    def over_z(v):
        v = lax.all_gather(v, "z", axis=0, tiled=True)
        return v.reshape(groups, GROUP * tok_count, width)

    rows = over_z(residuals)

    global_block = (routes[:, None] * BLOCKS + blocks).T.reshape(1, 4, tok_count)
    ids = lax.all_to_all(
        jnp.broadcast_to(global_block, (NZ, 4, tok_count)), "z", 0, 0, tiled=True
    )

    def tables(ids):
        here = ((ids >> 1) & 15) == z
        pick, turned = routing(jnp.where(here, (ids >> 5) * owned + (ids & 1), -1), LOCAL)
        present = jnp.sum(pick.astype(F32), axis=2).reshape(groups, LOCAL, -1)
        present = present.transpose(1, 0, 2).reshape(LOCAL, -1, 1)
        peers = jnp.arange(8, dtype=jnp.int32)
        return pick, turned, present, peer_place(peers >> 2, peers & 3)

    pieces, left = [], enc_bias
    for _ in range(3):
        piece = lax.reduce_precision(left, 8, 7)
        pieces.append(piece.astype(BF16))
        left = left - piece
    pieces = jnp.stack(pieces, 1)
    turned_enc = jnp.concatenate(
        [enc_weight.swapaxes(1, 2), jnp.pad(pieces, ((0, 0), (0, 13), (0, 0)))], axis=1
    )
    turned_enc = both(gather_half(turned_enc, (), lambda v: v)[0])
    dec_half, (pick, turned, present, order) = gather_half(dec_weight, ids, tables)
    bias_local = jnp.concatenate([w[:, width : width + 3] for w in turned_enc])
    bias_local = jnp.sum(bias_local.astype(F32)[:, ::-1], 1, keepdims=True)

    pick, bias_local = tie(pick, bias_local)
    pre_part, = project(order, pick, rows, *turned_enc, False)
    dec_local = both(dec_half)
    copies = lax.all_to_all(pre_part, "lat", 0, 0, tiled=True)
    pre, act, home = decode(order, copies, bias_local, turned, *dec_local)
    home, rows = tie(home, rows)
    total = lax.psum_scatter(
        home.reshape(NZ * tok_count, width), "z", scatter_dimension=0, tiled=True
    )

    owner_rows = to_owners(select(pick, rows))
    turned_dec = [w.swapaxes(1, 2) for w in dec_local]
    total, owner_rows, turned_dec = tie(total, owner_rows, turned_dec)
    recon = total.astype(F32) + dec_bias[None, :]
    reconstruction = recon.astype(BF16)
    error = (recon - residuals.astype(F32)).astype(BF16)
    errors = over_z(error)

    owner_act = to_owners(act)
    sig = jax.nn.sigmoid(pre) * present
    errors, owner_act, sig = tie(errors, owner_act, sig)

    error_slots = pick_slots(pick, errors)
    dact = inward(order, error_slots, *turned_dec)
    owner_errors = to_owners(error_slots)
    slope, owner_errors = tie(slopes(dact, sig), owner_errors)
    owner_slope = to_owners(slope)
    enc_grad, enc_bias_grad = outer(owner_slope, owner_rows)
    dec_grad, _ = outer(owner_act, owner_errors)
    return reconstruction, enc_grad, enc_bias_grad, dec_grad


def solution(mesh):
    fine = Mesh(mesh.devices.reshape(2, NY, NZ, 4), ("sect", "y", "z", "lat"))
    own = ("sect", "y", "z")
    return jax.shard_map(
        shards,
        mesh=fine,
        in_specs=(
            P(own, "lat"),
            P(own),
            P(own, None),
            P(own, None, "lat"),
            P(own, None),
            P(own, None, "lat"),
            P("lat"),
        ),
        out_specs=(
            P(own, "lat"),
            P(own, None, "lat"),
            P(own, None),
            P(own, None, "lat"),
        ),
        check_vma=False,
    )
```
